256 devices in a mesh: box: 64 (over y, z, x_lo), blk: 4 (over x_hi, core).
Axes of the slice: x: 4 (x_hi: 2, x_lo: 2; x = x_hi * 2 + x_lo), y: 4, z: 8, core: 2. Of those that a mesh axis runs over, the one named last changes fastest.
Arguments:
- panels: float32 [1024, 4, 256], P('box'), may hold values from 0 to 65, as said below
- self_blocks: float32 [1024, 256, 256], P('box'), may hold values from 0 to 8, as said below
- neighbors: int32 [1024, 8], P('box'), may hold values from 0 to 1023, as said below
- skeleton_one: int32 [1024, 128], P('box'), may hold values from 0 to 255, as said below
- count_one: int32 [1024], P('box'), may hold values from 64 to 128
- skeleton_two: int32 [512, 128], P('box'), may hold values from 0 to 255, as said below
- count_two: int32 [512], P('box'), may hold values from 64 to 128
- parent_at_slot: int32 [512], P('box'), may hold values from 0 to 511, as said below
Outputs:
- level_one: float32 [1024, 128, 128], P('box', 'blk')
- level_two: float32 [512, 128, 128], P('box', 'blk')
The draws below stay inside these ranges and needn't reach their ends.
Inputs may be any that keep to these rules, and one draw needn't show every extreme that they name: `neighbors`: each box's 8 neighbours are distinct other boxes whose index differs from its own by at most 16; one of them differs by exactly 16. `skeleton_one`: each row lists 128 distinct panel positions. `skeleton_two`: each row lists 128 distinct positions. `parent_at_slot`: a permutation of the parents. `panels`: self terms (component 3) are 1 or more. `self_blocks`: diagonal entries equal the panels' self terms; the other entries are positive.
All inputs are finite; a program needn't handle non-finite values. Where the reference program divides by a largest or mean magnitude, that divisor is 1e-20 or more.
Results may differ from the reference program's by a relative error of at most 0.0003.
Values sent between devices are 32-bit elements; how exact they have to be, the bound alone decides.
A program may use at most 128 MiB of HBM per device.

```python
import jax
import jax.numpy as jnp
from jax import lax

P_SIZE = 256
K = 128
KMIN = 64
NB = 8
STEPS = 3
BOX_DEV = 16
BOXES = 1024
PARENTS = 512


def raw_geometry(key):
    key_offset, key_self = jax.random.split(key)
    offsets = jax.random.uniform(key_offset, (BOXES, 3, P_SIZE), jnp.float32)
    self_raw = jax.random.uniform(key_self, (BOXES, P_SIZE), jnp.float32)
    box_ids = jnp.arange(BOXES)
    centres = jnp.stack([box_ids % 4, box_ids // 4 % 4, box_ids // 16], 1).astype(jnp.float32)
    return (offsets, self_raw, centres)


def draw_panels(key, part):
    offsets, self_raw, centres = raw_geometry(key)
    self_term = jnp.exp(jnp.log(8.0) * self_raw)
    coords = centres[:, :, None] + 0.9 * offsets
    return jnp.concatenate([coords, self_term[:, None, :]], 1)


def draw_self_blocks(key, part):
    offsets, self_raw, centres = raw_geometry(key)
    key = jax.random.fold_in(key, 2)
    self_term = jnp.exp(jnp.log(8.0) * self_raw)
    coords = centres[:, :, None] + 0.9 * offsets
    parts = []
    for axis_id in range(3):
        offset = coords[:, axis_id, :, None] - coords[:, axis_id, None, :]
        parts.append(offset * offset)
    rough = 1.0 + 0.5 * jax.random.uniform(key, (BOXES, P_SIZE, P_SIZE), jnp.float32, -1.0, 1.0)
    values = 0.03125 / jnp.sqrt(parts[0] + parts[1] + parts[2] + 0.01) * rough
    diagonal = jnp.arange(P_SIZE)[:, None] == jnp.arange(P_SIZE)[None, :]
    return jnp.where(diagonal[None], self_term[:, :, None], values)


def draw_neighbors(key, part):
    key = jax.random.fold_in(key, 3)
    box_ids = jnp.arange(BOXES)
    shifts = jnp.concatenate([jnp.arange(-BOX_DEV, 0), jnp.arange(1, BOX_DEV + 1)])
    candidates = box_ids[:, None] + shifts[None, :]
    inside = (candidates >= 0) & (candidates < BOXES)
    forced_shift = jnp.where(box_ids + BOX_DEV < BOXES, BOX_DEV, -BOX_DEV)
    forced = shifts[None, :] == forced_shift[:, None]
    scores = jax.random.randint(key, (BOXES, 2 * BOX_DEV), 0, 65536) * (2 * BOX_DEV) + jnp.arange(2 * BOX_DEV)[None, :]
    scores = jnp.where(forced, 1073741824, jnp.where(inside, scores, -1))
    top_vals, positions = lax.top_k(scores, NB)
    return jnp.take_along_axis(candidates, positions, 1).astype(jnp.int32)


def distinct_rows(key, rows, choices, count):
    scores = jax.random.randint(key, (rows, choices), 0, 65536) * choices + jnp.arange(choices)[None, :]
    return jnp.argsort(scores, axis=1, stable=True)[:, :count].astype(jnp.int32)


def ragged_counts(key, rows):
    key_main, key_high, key_low = jax.random.split(key, 3)
    counts = jax.random.randint(key_main, (rows,), KMIN, K + 1)
    high_pos = jax.random.randint(key_high, (), 0, rows)
    low_pos = (high_pos + jax.random.randint(key_low, (), 1, rows)) % rows
    return counts.at[high_pos].set(K).at[low_pos].set(KMIN).astype(jnp.int32)


def draw_skeleton_one(key, part):
    key = jax.random.fold_in(key, 4)
    return distinct_rows(key, BOXES, P_SIZE, K)


def draw_count_one(key, part):
    key = jax.random.fold_in(key, 5)
    return ragged_counts(key, BOXES)


def draw_skeleton_two(key, part):
    key = jax.random.fold_in(key, 6)
    return distinct_rows(key, PARENTS, 2 * K, K)


def draw_count_two(key, part):
    key = jax.random.fold_in(key, 7)
    return ragged_counts(key, PARENTS)


def draw_parent_at_slot(key, part):
    key = jax.random.fold_in(key, 8)
    key_order, key_dev, key_slot, key_want = jax.random.split(key, 4)
    order = distinct_rows(key_order, 1, PARENTS, PARENTS)[0]
    half_box = BOX_DEV // 2
    owner_count = BOXES // BOX_DEV
    device_id = jax.random.randint(key_dev, (), 0, owner_count)
    first_slot = device_id * half_box + jax.random.randint(key_slot, (), 0, half_box)
    wanted = (device_id + owner_count // 2) % owner_count * half_box + jax.random.randint(key_want, (), 0, half_box)
    where_wanted = jnp.argmax((order == wanted).astype(jnp.int32))
    previous = order[first_slot]
    order = order.at[where_wanted].set(previous).at[first_slot].set(wanted)
    return order.astype(jnp.int32)


def setup_inputs(seed: int = 0) -> dict:
    streams_of = jax.random.split(jax.random.key(seed), 9)
    return {
        "panels": draw_panels(jax.random.fold_in(streams_of[8], 71), 0),
        "self_blocks": draw_self_blocks(jax.random.fold_in(streams_of[8], 71), 0),
        "neighbors": draw_neighbors(jax.random.fold_in(streams_of[8], 71), 0),
        "skeleton_one": draw_skeleton_one(jax.random.fold_in(streams_of[8], 71), 0),
        "count_one": draw_count_one(jax.random.fold_in(streams_of[8], 71), 0),
        "skeleton_two": draw_skeleton_two(jax.random.fold_in(streams_of[8], 71), 0),
        "count_two": draw_count_two(jax.random.fold_in(streams_of[8], 71), 0),
        "parent_at_slot": draw_parent_at_slot(jax.random.fold_in(streams_of[8], 71), 0),
    }


precise = lax.Precision.HIGHEST

def kernel(source, target):
    parts = []
    for axis_id in range(3):
        offset = source[..., axis_id, :, None] - target[..., axis_id, None, :]
        parts.append(offset * offset)
    return 0.03125 / jnp.sqrt(parts[0] + parts[1] + parts[2] + 0.01)

def normal_terms(proxy_kernel, skeleton, live_mask):
    picked_cols = jnp.take(proxy_kernel, skeleton, axis=1) * live_mask[None, :]
    gram_part = jnp.dot(picked_cols.T, picked_cols, precision=precise)
    right_part = jnp.dot(picked_cols.T, proxy_kernel, precision=precise)
    return (gram_part, right_part)

def refine(gram_part, right_part, skeleton, live_mask):
    step_size = 1.0 / lax.optimization_barrier(jnp.max(lax.optimization_barrier(jnp.sum(jnp.abs(gram_part), axis=-1)), axis=-1))
    fits = jax.nn.one_hot(skeleton, right_part.shape[-1], dtype=jnp.float32) * live_mask[..., None]
    for sweep in range(STEPS):
        update = right_part - jnp.einsum('...kl,...lp->...kp', gram_part, fits, precision=precise)
        fits = fits + jnp.asarray(step_size)[..., None, None] * update
    return fits

def reference(panels, self_blocks, neighbors, skeleton_one, count_one, skeleton_two, count_two, parent_at_slot):
    slot_ids = jnp.arange(K)

    def leaf_fit(box_id):
        near_pts = panels[neighbors[box_id], :3]
        proxy = jnp.transpose(near_pts, (1, 0, 2)).reshape(3, -1)
        proxy_kernel = kernel(proxy, panels[box_id, :3])
        live_mask = (slot_ids < count_one[box_id]).astype(jnp.float32)
        gram_part, right_part = normal_terms(proxy_kernel, skeleton_one[box_id], live_mask)
        return refine(gram_part, right_part, skeleton_one[box_id], live_mask)
    fits = lax.map(leaf_fit, jnp.arange(BOXES))
    weights = jnp.maximum(jnp.einsum('bkp,bp->bk', fits * fits, panels[:, 3], precision=precise), 1.0)

    def coarse(box_id):
        own_fit = fits[box_id]
        block_rows = jnp.dot(jnp.dot(own_fit, self_blocks[box_id], precision=precise), own_fit.T, precision=precise)
        near_ids = neighbors[box_id]
        couple = kernel(panels[box_id, :3], panels[near_ids, :3])
        left_prod = jnp.einsum('kp,npq->nkq', own_fit, couple, precision=precise)
        cross_block = jnp.einsum('nkq,nlq->nkl', left_prod, fits[near_ids], precision=precise)
        schur_term = jnp.einsum('nkl,nml->km', cross_block / weights[near_ids][:, None, :], cross_block, precision=precise)
        return block_rows - schur_term
    level_one = lax.map(coarse, jnp.arange(BOXES))

    def level_fit(slot_id):
        parent_id = parent_at_slot[slot_id]
        first = 2 * parent_id
        second = first + 1
        couple = kernel(panels[first, :3], panels[second, :3])
        cross_block = jnp.dot(jnp.dot(fits[first], couple, precision=precise), fits[second].T, precision=precise)
        merged = jnp.concatenate([jnp.concatenate([level_one[first], cross_block], 1), jnp.concatenate([cross_block.T, level_one[second]], 1)], 0)
        live_mask = (slot_ids < count_two[slot_id]).astype(jnp.float32)
        gram_part, right_part = normal_terms(merged, skeleton_two[slot_id], live_mask)
        inner_fit = refine(gram_part, right_part, skeleton_two[slot_id], live_mask)
        return jnp.dot(jnp.dot(inner_fit, merged, precision=precise), inner_fit.T, precision=precise)
    level_two = lax.map(level_fit, jnp.arange(PARENTS))
    return (level_one, level_two)
```

```python
import functools

import jax
import jax.numpy as jnp
from jax import lax
from jax.experimental import pallas as pl
from jax.experimental.pallas import tpu as pltpu
from jax.sharding import PartitionSpec as P

STEPS = 3
MESH = pl.DeviceIdType.MESH
F32 = jnp.float32
BF16 = jnp.bfloat16
NN = (((1,), (0,)), ((), ()))
NT = (((1,), (1,)), ((), ()))
TN = (((0,), (0,)), ((), ()))
MIB = 1 << 20

HOMES, MEMBERS = 64, 4
BOXES, MINE = 16, 4
PANELS, SLOTS, NEAR = 256, 128, 8
UNITS = HOMES * 2
Z, W = 8, 8
PARENTS = 512
ROWS = SLOTS // MEMBERS


def halves(x):
    high = x.astype(BF16)
    return high, (x - high.astype(F32)).astype(BF16)


def dot(a, b, dims):
    return lax.dot_general(a, b, dims, preferred_element_type=F32)


def dot3(a, b, dims):
    return dot(a[0], b[0], dims) + (dot(a[0], b[1], dims) + dot(a[1], b[0], dims))


def square(a, dims):
    cross = dot(a[0], a[1], dims)
    return dot(a[0], a[0], dims) + (cross + cross.T)


def place():
    home, member = lax.axis_index("box"), lax.axis_index("blk")
    return home, member


def enter(peers):
    barrier = pltpu.get_barrier_semaphore()
    for peer in peers:
        pl.semaphore_signal(barrier, inc=1, device_id=peer, device_id_type=MESH)
    pl.semaphore_wait(barrier, len(peers))


def send(source, target, send_sem, recv_sem, peer):
    return pltpu.make_async_remote_copy(
        src_ref=source,
        dst_ref=target,
        send_sem=send_sem,
        recv_sem=recv_sem,
        device_id=peer,
        device_id_type=MESH,
    )


def halo_kernel(panels, window, own_sem, send_sem, recv_sem):
    home, member = place()
    after = (lax.rem(home + 1, HOMES), member)
    before = (lax.rem(home + HOMES - 1, HOMES), member)
    enter((after, before))
    up = send(panels, window.at[pl.ds(0, BOXES)], send_sem.at[0], recv_sem.at[0], after)
    down = send(panels, window.at[pl.ds(2 * BOXES, BOXES)], send_sem.at[1], recv_sem.at[1], before)
    own = pltpu.make_async_copy(panels, window.at[pl.ds(BOXES, BOXES)], own_sem)
    up.start()
    down.start()
    own.start()
    own.wait()
    up.wait()
    down.wait()


def halo(panels):
    return pl.pallas_call(
        halo_kernel,
        out_shape=jax.ShapeDtypeStruct((3 * BOXES, 4, PANELS), F32),
        in_specs=[pl.BlockSpec(memory_space=pl.ANY)],
        out_specs=pl.BlockSpec(memory_space=pl.ANY),
        scratch_shapes=[
            pltpu.SemaphoreType.DMA,
            pltpu.SemaphoreType.DMA((2,)),
            pltpu.SemaphoreType.DMA((2,)),
        ],
        compiler_params=pltpu.CompilerParams(collective_id=0, has_side_effects=True),
        name="halo",
    )(panels)


def refine(gram, right, chosen):
    steps = [1.0 / jnp.max(jnp.sum(jnp.abs(g), axis=1, keepdims=True), axis=0, keepdims=True) for g in gram]
    grams = [halves(g) for g in gram]
    fits = list(chosen)
    for _ in range(STEPS):
        updates = [r - dot3(g, halves(f), NN) for g, r, f in zip(grams, right, fits)]
        fits = [f + s * u for f, s, u in zip(fits, steps, updates)]
    return fits


def chosen_columns(row, count):
    position = lax.broadcasted_iota(jnp.int32, (2 * SLOTS, SLOTS), 0)
    slot = lax.broadcasted_iota(jnp.int32, (2 * SLOTS, SLOTS), 1)
    return jnp.where((position == row) & (slot < count), 1.0, 0.0).astype(F32)


def normal(square_matrix, columns):
    picks = columns.T
    picks16 = picks.astype(BF16)
    columns16 = columns.astype(BF16)
    high, low = halves(square_matrix)
    right = dot(picks16, high, NN) + dot(picks16, low, NN)
    high, low = halves(right)
    gram = dot(high, columns16, NN) + dot(low, columns16, NN)
    return gram, right, picks


def couple(col, row):
    total = None
    for axis in range(3):
        offset = col[axis] - row[axis]
        total = offset * offset if total is None else total + offset * offset
    return 0.03125 * lax.rsqrt(total + 0.01)


def fit_kernel(
    ids, near, count, window, skeleton, blocks, fitw_out, left_out, block_out, pair_out, column, high, low, sums
):
    home, member = ids[0], ids[1]
    base = (home - 1) * BOXES
    first = member * MINE
    tile = 64

    def fill(own, box, lane, write):
        for part in range(PANELS // SLOTS):
            lanes = slice(part * SLOTS, (part + 1) * SLOTS)
            row = [window[box, axis : axis + 1, lanes] for axis in range(3)]
            for start in range(0, PANELS, tile):
                col = [column[own, axis, start : start + tile, :] for axis in range(3)]
                hi, lo = halves(couple(col, row))
                write(start, part, hi, lo)

    for own in range(MINE):
        for axis in range(3):
            row = window[BOXES + first + own, axis : axis + 1, :]
            column[own, axis] = jnp.broadcast_to(row, (SLOTS, PANELS)).T

    def proxies(own, _):
        def one(index, _):
            box = near[first + own, index] - base

            def write(start, part, hi, lo):
                lanes = pl.ds(pl.multiple_of(index * PANELS + part * SLOTS, SLOTS), SLOTS)
                high[own, start : start + tile, lanes] = hi
                low[own, start : start + tile, lanes] = lo

            fill(own, box, None, write)
            return 0

        lax.fori_loop(0, NEAR, one, 0)
        sums[own] = square((high[own], low[own]), NT)
        return 0

    lax.fori_loop(0, MINE, proxies, 0)

    grams, rights, picks = [], [], []
    for own in range(MINE):
        columns = chosen_columns(skeleton[pl.ds(first + own, 1), :], count[first + own])
        gram, right, pick = normal(sums[own], columns)
        grams.append(gram)
        rights.append(right)
        picks.append(pick)
    fits = refine(grams, rights, picks)
    split = [halves(fit) for fit in fits]
    for own in range(MINE):
        self_term = window[BOXES + first + own, 3:4, :]
        weight = jnp.maximum(jnp.sum(fits[own] * fits[own] * self_term, axis=1, keepdims=True), 1.0)
        fitw_out[own] = fits[own] * lax.rsqrt(weight)
    for own in range(MINE):
        part = dot3(split[own], halves(blocks[own]), NN)
        block_out[own] = dot3(halves(part), split[own], NT)
    for own in range(MINE):
        for index in range(NEAR):
            lanes = slice(index * PANELS, (index + 1) * PANELS)
            left_out[own, :, lanes] = dot3(split[own], (high[own, :, lanes], low[own, :, lanes]), NN)
    for pair in range(MINE // 2):
        a, e = 2 * pair, 2 * pair + 1

        def write(start, part, hi, lo):
            lanes = slice(part * SLOTS, (part + 1) * SLOTS)
            high[a, start : start + tile, lanes] = hi
            low[a, start : start + tile, lanes] = lo

        fill(a, BOXES + first + e, None, write)
        part = dot3(split[a], (high[a, :, :PANELS], low[a, :, :PANELS]), NN)
        pair_out[pair] = dot3(halves(part), split[e], NT)


def whole(shape):
    return pl.BlockSpec(shape, lambda *_: (0,) * len(shape))


def fit_call(ids, near, count, window, skeleton, blocks):
    return pl.pallas_call(
        fit_kernel,
        grid_spec=pltpu.PrefetchScalarGridSpec(
            num_scalar_prefetch=3,
            grid=(1,),
            in_specs=[
                whole((3 * BOXES, 4, PANELS)),
                whole((BOXES, SLOTS)),
                pl.BlockSpec((MINE, PANELS, PANELS), lambda i, ids, *_: (ids[1], 0, 0)),
            ],
            out_specs=[
                whole((MINE, SLOTS, PANELS)),
                whole((MINE, SLOTS, NEAR * PANELS)),
                whole((MINE, SLOTS, SLOTS)),
                whole((MINE // 2, SLOTS, SLOTS)),
            ],
            scratch_shapes=[
                pltpu.VMEM((MINE, 3, PANELS, SLOTS), F32),
                pltpu.VMEM((MINE, PANELS, NEAR * PANELS), BF16),
                pltpu.VMEM((MINE, PANELS, NEAR * PANELS), BF16),
                pltpu.VMEM((MINE, PANELS, PANELS), F32),
            ],
        ),
        out_shape=[
            jax.ShapeDtypeStruct((MINE, SLOTS, PANELS), F32),
            jax.ShapeDtypeStruct((MINE, SLOTS, NEAR * PANELS), F32),
            jax.ShapeDtypeStruct((MINE, SLOTS, SLOTS), F32),
            jax.ShapeDtypeStruct((MINE // 2, SLOTS, SLOTS), F32),
        ],
        compiler_params=pltpu.CompilerParams(vmem_limit_bytes=56 * MIB),
        name="fit",
    )(ids, near, count, window, skeleton, blocks)


def exchange_kernel(fits, window, own_sem, send_sem, recv_sem, pass_sem, take_sem):
    home, member = place()
    side, core = member // 2, lax.rem(member, 2)
    unit = 2 * home + side

    def chip(shift):
        other = lax.rem(unit + shift + UNITS, UNITS)
        return (other // 2, 2 * lax.rem(other, 2) + core)

    sibling = (home, 2 * side + 1 - core)
    shifts = (1, -1, 2, -2)
    enter([sibling] + [chip(shift) for shift in shifts])

    def slot(shift):
        return window.at[2 * (2 + shift) + core]

    own = pltpu.make_async_copy(fits, slot(0), own_sem)
    sends = [
        send(fits, slot(-shift), send_sem.at[i], recv_sem.at[i], chip(shift)) for i, shift in enumerate(shifts)
    ]
    passes = [send(fits, slot(0), pass_sem.at[4], take_sem.at[4], sibling)] + [
        send(slot(-shift), slot(-shift), pass_sem.at[i], take_sem.at[i], sibling) for i, shift in enumerate(shifts)
    ]
    for copy in sends:
        copy.start()
    passes[0].start()
    own.start()
    for i in range(4):
        sends[i].wait_recv()
        passes[1 + i].start()
    own.wait()
    for copy in sends:
        copy.wait_send()
    for copy in passes:
        copy.wait()


def exchange(fits):
    return pl.pallas_call(
        exchange_kernel,
        out_shape=jax.ShapeDtypeStruct((10, MINE, SLOTS, PANELS), F32),
        in_specs=[pl.BlockSpec(memory_space=pl.ANY)],
        out_specs=pl.BlockSpec(memory_space=pl.ANY),
        scratch_shapes=[
            pltpu.SemaphoreType.DMA,
            pltpu.SemaphoreType.DMA((4,)),
            pltpu.SemaphoreType.DMA((4,)),
            pltpu.SemaphoreType.DMA((5,)),
            pltpu.SemaphoreType.DMA((5,)),
        ],
        compiler_params=pltpu.CompilerParams(collective_id=1, has_side_effects=True),
        name="exchange",
    )(fits)


def level_kernel(ids, near, count, fitw, left, block, pair, owners, skeleton, one_out, two_out, high, low, merged):
    home, member = ids[0], ids[1]
    first = member * MINE
    base = 16 * home + 8 * (member // 2) - 16

    for own in range(MINE):
        for index in range(NEAR):
            box = near[first + own, index] - base
            lanes = slice(index * PANELS, (index + 1) * PANELS)
            hi, lo = halves(dot3(halves(left[own, :, lanes]), halves(fitw[box]), NT))
            high[own, :, index * SLOTS : (index + 1) * SLOTS] = hi
            low[own, :, index * SLOTS : (index + 1) * SLOTS] = lo
        one_out[own] = block[own] - square((high[own], low[own]), NT)
    grams, rights, picks, bodies = [], [], [], []
    for j in range(MINE // 2):
        cross = pair[j]
        merged[j, :SLOTS, :SLOTS] = one_out[2 * j]
        merged[j, :SLOTS, SLOTS:] = cross
        merged[j, SLOTS:, :SLOTS] = cross.T
        merged[j, SLOTS:, SLOTS:] = one_out[2 * j + 1]
        body = halves(merged[j])
        parent = (home * BOXES + first) // 2 + j
        order = (
            lax.broadcasted_iota(jnp.int32, owners.shape, 0) * SLOTS
            + lax.broadcasted_iota(jnp.int32, owners.shape, 1)
        ).astype(F32)
        slot = jnp.sum(jnp.where(owners[...] == parent, order, 0.0)).astype(jnp.int32)
        columns = chosen_columns(skeleton[pl.ds(slot, 1), :], count[slot])
        gram, right, pick = normal(square(body, TN), columns)
        grams.append(gram)
        rights.append(right)
        picks.append(pick)
        bodies.append(body)
    fits = refine(grams, rights, picks)
    for j in range(MINE // 2):
        fit = halves(fits[j])
        two_out[j] = dot3(halves(dot3(fit, bodies[j], NN)), fit, NT)


def level_call(ids, near, count, fitw, left, block, pair, owners, skeleton):
    return pl.pallas_call(
        level_kernel,
        grid_spec=pltpu.PrefetchScalarGridSpec(
            num_scalar_prefetch=3,
            grid=(1,),
            in_specs=[
                whole(fitw.shape),
                whole(left.shape),
                whole(block.shape),
                whole(pair.shape),
                whole(owners.shape),
                whole(skeleton.shape),
            ],
            out_specs=[whole((MINE, SLOTS, SLOTS)), whole((MINE // 2, SLOTS, SLOTS))],
            scratch_shapes=[
                pltpu.VMEM((MINE, SLOTS, NEAR * SLOTS), BF16),
                pltpu.VMEM((MINE, SLOTS, NEAR * SLOTS), BF16),
                pltpu.VMEM((MINE // 2, PANELS, PANELS), F32),
            ],
        ),
        out_shape=[
            jax.ShapeDtypeStruct((MINE, SLOTS, SLOTS), F32),
            jax.ShapeDtypeStruct((MINE // 2, SLOTS, SLOTS), F32),
        ],
        compiler_params=pltpu.CompilerParams(vmem_limit_bytes=56 * MIB),
        name="level",
    )(ids, near, count, fitw, left, block, pair, owners, skeleton)


def route_kernel(
    owners, one, two, one_out, two_out, lines, packed, arrived,
    own_sem, row_send, row_recv, block_send, block_recv, line_send, line_recv, plane_send, plane_recv,
):
    home, member = place()
    across = 2 * (home // 16) + lax.rem(home, 2)
    along = lax.rem(home // 2, Z)

    def home_at(across_at, along_at):
        return (across_at // 2) * 16 + along_at * 2 + lax.rem(across_at, 2)

    members = [(home, lax.rem(member + d, MEMBERS)) for d in range(1, MEMBERS)]
    line = [(home_at(across, lax.rem(along + d, Z)), member) for d in range(1, Z)]
    plane_at = [lax.rem(across + d, W) for d in range(1, W)]
    plane = [(home_at(at, along), member) for at in plane_at]
    enter(members + line + plane)

    def rows(array, target):
        return array.at[:, pl.ds(pl.multiple_of(target * ROWS, ROWS), ROWS), :]

    ours = lines.at[along]
    own_two = pltpu.make_async_copy(rows(two, member), ours.at[pl.ds(2 * member, 2)], own_sem.at[0])
    own_one = pltpu.make_async_copy(rows(one, member), one_out.at[pl.ds(MINE * member, MINE)], own_sem.at[1])
    blocks = [
        send(rows(two, peer[1]), ours.at[pl.ds(2 * member, 2)], block_send.at[i], block_recv.at[i], peer)
        for i, peer in enumerate(members)
    ]
    ones = [
        send(rows(one, peer[1]), one_out.at[pl.ds(MINE * member, MINE)], row_send.at[i], row_recv.at[i], peer)
        for i, peer in enumerate(members)
    ]
    for copy in blocks:
        copy.start()
    own_two.start()
    own_one.start()
    for copy in ones:
        copy.start()
    own_two.wait()
    for copy in blocks:
        copy.wait_recv()
    gathers = [send(ours, ours, line_send.at[i], line_recv.at[i], peer) for i, peer in enumerate(line)]
    for copy in gathers:
        copy.start()
    for copy in gathers:
        copy.wait_recv()

    def pack(target, at):
        to = home_at(at, along)
        for s in range(8):
            parent = owners[8 * to + s]
            source = parent // 8
            target[s] = lines[lax.rem(source // 2, Z), lax.rem(parent, 8)]

    sends = []
    for i, peer in enumerate(plane):
        pack(packed.at[i], plane_at[i])
        copy = send(packed.at[i], arrived.at[across], plane_send.at[i], plane_recv.at[i], peer)
        copy.start()
        sends.append(copy)
    pack(arrived.at[across], across)
    for copy in sends:
        copy.wait_recv()
    for s in range(8):
        source = owners[8 * home + s] // 8
        two_out[s] = arrived[2 * (source // 16) + lax.rem(source, 2), s]
    own_one.wait()
    for copy in ones:
        copy.wait()
    for copy in blocks + gathers + sends:
        copy.wait_send()


def route(owners, one, two):
    dma = pltpu.SemaphoreType.DMA
    return pl.pallas_call(
        route_kernel,
        out_shape=[
            jax.ShapeDtypeStruct((BOXES, ROWS, SLOTS), F32),
            jax.ShapeDtypeStruct((8, ROWS, SLOTS), F32),
        ],
        in_specs=[
            pl.BlockSpec(memory_space=pltpu.SMEM),
            pl.BlockSpec(memory_space=pl.ANY),
            pl.BlockSpec(memory_space=pl.ANY),
        ],
        out_specs=[pl.BlockSpec(memory_space=pl.ANY), pl.BlockSpec(memory_space=pltpu.VMEM)],
        scratch_shapes=[
            pltpu.VMEM((Z, 8, ROWS, SLOTS), F32),
            pltpu.VMEM((W - 1, 8, ROWS, SLOTS), F32),
            pltpu.VMEM((W, 8, ROWS, SLOTS), F32),
            dma((2,)), dma((3,)), dma((3,)), dma((3,)), dma((3,)),
            dma((Z - 1,)), dma((Z - 1,)), dma((W - 1,)), dma((W - 1,)),
        ],
        compiler_params=pltpu.CompilerParams(collective_id=2, has_side_effects=True),
        name="route",
    )(owners, one, two)


def local(panels, self_blocks, neighbors, skeleton_one, count_one, skeleton_two, count_two, parent_at_slot):
    home, member = place()
    ids = jnp.stack([home, member]).astype(jnp.int32)
    owners = lax.all_gather(parent_at_slot, "box", axis=0, tiled=True)
    counts = lax.all_gather(count_two, "box", axis=0, tiled=True)
    skeletons = lax.all_gather(skeleton_two, "box", axis=0, tiled=True)
    window = halo(panels)
    fitw, left, block, pair = fit_call(ids, neighbors, count_one, window, skeleton_one, self_blocks)
    reach = exchange(fitw).reshape(10 * MINE, SLOTS, PANELS)
    one, two = level_call(
        ids, neighbors, counts, reach, left, block, pair, owners.reshape(4, SLOTS), skeletons
    )
    return route(owners, one, two)


def solution(mesh):
    placed = (
        P("box", None, None),
        P("box", None, None),
        P("box", None),
        P("box", None),
        P("box"),
        P("box", None),
        P("box"),
        P("box"),
    )
    return jax.shard_map(
        local,
        mesh=mesh,
        in_specs=placed,
        out_specs=(P("box", "blk", None), P("box", "blk", None)),
        check_vma=False,
    )
```

```python
import functools

import jax
import jax.numpy as jnp
from jax import lax
from jax.experimental import pallas as pl
from jax.experimental.pallas import tpu as pltpu
from jax.sharding import PartitionSpec as P

STEPS = 3
MESH = pl.DeviceIdType.MESH
F32 = jnp.float32
BF16 = jnp.bfloat16
NN = (((1,), (0,)), ((), ()))
NT = (((1,), (1,)), ((), ()))
TN = (((0,), (0,)), ((), ()))
MIB = 1 << 20

HOMES, MEMBERS = 64, 4
BOXES, MINE = 16, 4
PANELS, SLOTS, NEAR = 256, 128, 8
UNITS = HOMES * 2
Z, W = 8, 8
PARENTS = 512
ROWS = SLOTS // MEMBERS
PARTS = 2


def halves(x):
    high = x.astype(BF16)
    return high, (x - high.astype(F32)).astype(BF16)


def dot(a, b, dims):
    return lax.dot_general(a, b, dims, preferred_element_type=F32)


def dot3(a, b, dims):
    return dot(a[0], b[0], dims) + (dot(a[0], b[1], dims) + dot(a[1], b[0], dims))


def square(a, dims):
    cross = dot(a[0], a[1], dims)
    return dot(a[0], a[0], dims) + (cross + cross.T)


def place():
    home, member = lax.axis_index("box"), lax.axis_index("blk")
    return home, member


def enter(peers):
    barrier = pltpu.get_barrier_semaphore()
    for peer in peers:
        pl.semaphore_signal(barrier, inc=1, device_id=peer, device_id_type=MESH)
    pl.semaphore_wait(barrier, len(peers))


def send(source, target, send_sem, recv_sem, peer):
    return pltpu.make_async_remote_copy(
        src_ref=source,
        dst_ref=target,
        send_sem=send_sem,
        recv_sem=recv_sem,
        device_id=peer,
        device_id_type=MESH,
    )


def home_at(across, along):
    return (across // 2) * 16 + along * 2 + lax.rem(across, 2)


def lines_of(home, member):
    across = 2 * (home // 16) + lax.rem(home, 2)
    along = lax.rem(home // 2, Z)
    line = [(home_at(across, lax.rem(along + d, Z)), member) for d in range(1, Z)]
    spots = [lax.rem(across + d, W) for d in range(1, W)]
    plane = [(spot, (home_at(spot, along), member)) for spot in spots]
    return line, plane, across, along


def halo_kernel(panels, window, own_sem, send_sem, recv_sem):
    home, member = place()
    after = (lax.rem(home + 1, HOMES), member)
    before = (lax.rem(home + HOMES - 1, HOMES), member)
    enter((after, before))
    up = send(panels, window.at[pl.ds(0, BOXES)], send_sem.at[0], recv_sem.at[0], after)
    down = send(panels, window.at[pl.ds(2 * BOXES, BOXES)], send_sem.at[1], recv_sem.at[1], before)
    own = pltpu.make_async_copy(panels, window.at[pl.ds(BOXES, BOXES)], own_sem)
    up.start()
    down.start()
    own.start()
    own.wait()
    up.wait()
    down.wait()


def halo(panels):
    return pl.pallas_call(
        halo_kernel,
        out_shape=jax.ShapeDtypeStruct((3 * BOXES, 4, PANELS), F32),
        in_specs=[pl.BlockSpec(memory_space=pl.ANY)],
        out_specs=pl.BlockSpec(memory_space=pl.ANY),
        scratch_shapes=[
            pltpu.SemaphoreType.DMA,
            pltpu.SemaphoreType.DMA((2,)),
            pltpu.SemaphoreType.DMA((2,)),
        ],
        compiler_params=pltpu.CompilerParams(collective_id=0, has_side_effects=True),
        name="halo",
    )(panels)


def refine(gram, right, chosen):
    steps = [1.0 / jnp.max(jnp.sum(jnp.abs(g), axis=1, keepdims=True), axis=0, keepdims=True) for g in gram]
    grams = [halves(g) for g in gram]
    fits = list(chosen)
    for _ in range(STEPS):
        updates = [r - dot3(g, halves(f), NN) for g, r, f in zip(grams, right, fits)]
        fits = [f + s * u for f, s, u in zip(fits, steps, updates)]
    return fits


def chosen_columns(row, count):
    position = lax.broadcasted_iota(jnp.int32, (2 * SLOTS, SLOTS), 0)
    slot = lax.broadcasted_iota(jnp.int32, (2 * SLOTS, SLOTS), 1)
    return jnp.where((position == row) & (slot < count), 1.0, 0.0).astype(F32)


def normal(square_matrix, columns):
    picks = columns.T
    picks16 = picks.astype(BF16)
    columns16 = columns.astype(BF16)
    high, low = halves(square_matrix)
    right = dot(picks16, high, NN) + dot(picks16, low, NN)
    high, low = halves(right)
    gram = dot(high, columns16, NN) + dot(low, columns16, NN)
    return gram, right, picks


def couple(col, row):
    total = None
    for axis in range(3):
        offset = col[axis] - row[axis]
        total = offset * offset if total is None else total + offset * offset
    return 0.03125 * lax.rsqrt(total + 0.01)


def fit_kernel(
    ids, near, count, window, skeleton, blocks, fitw_out, left_out, block_out, pair_out, column, high, low, sums
):
    home, member = ids[0], ids[1]
    base = (home - 1) * BOXES
    first = member * MINE
    tile = 64

    def fill(own, box, lane, write):
        for part in range(PANELS // SLOTS):
            lanes = slice(part * SLOTS, (part + 1) * SLOTS)
            row = [window[box, axis : axis + 1, lanes] for axis in range(3)]
            for start in range(0, PANELS, tile):
                col = [column[own, axis, start : start + tile, :] for axis in range(3)]
                hi, lo = halves(couple(col, row))
                write(start, part, hi, lo)

    for own in range(MINE):
        for axis in range(3):
            row = window[BOXES + first + own, axis : axis + 1, :]
            column[own, axis] = jnp.broadcast_to(row, (SLOTS, PANELS)).T

    def proxies(own, _):
        def one(index, _):
            box = near[first + own, index] - base

            def write(start, part, hi, lo):
                lanes = pl.ds(pl.multiple_of(index * PANELS + part * SLOTS, SLOTS), SLOTS)
                high[own, start : start + tile, lanes] = hi
                low[own, start : start + tile, lanes] = lo

            fill(own, box, None, write)
            return 0

        lax.fori_loop(0, NEAR, one, 0)
        sums[own] = square((high[own], low[own]), NT)
        return 0

    lax.fori_loop(0, MINE, proxies, 0)

    grams, rights, picks = [], [], []
    for own in range(MINE):
        columns = chosen_columns(skeleton[pl.ds(first + own, 1), :], count[first + own])
        gram, right, pick = normal(sums[own], columns)
        grams.append(gram)
        rights.append(right)
        picks.append(pick)
    fits = refine(grams, rights, picks)
    split = [halves(fit) for fit in fits]
    for own in range(MINE):
        self_term = window[BOXES + first + own, 3:4, :]
        weight = jnp.maximum(jnp.sum(fits[own] * fits[own] * self_term, axis=1, keepdims=True), 1.0)
        fitw_out[own] = fits[own] * lax.rsqrt(weight)
    for own in range(MINE):
        part = dot3(split[own], halves(blocks[own]), NN)
        block_out[own] = dot3(halves(part), split[own], NT)
    for own in range(MINE):
        for index in range(NEAR):
            lanes = slice(index * PANELS, (index + 1) * PANELS)
            left_out[own, :, lanes] = dot3(split[own], (high[own, :, lanes], low[own, :, lanes]), NN)
    for pair in range(MINE // 2):
        a, e = 2 * pair, 2 * pair + 1

        def write(start, part, hi, lo):
            lanes = slice(part * SLOTS, (part + 1) * SLOTS)
            high[a, start : start + tile, lanes] = hi
            low[a, start : start + tile, lanes] = lo

        fill(a, BOXES + first + e, None, write)
        part = dot3(split[a], (high[a, :, :PANELS], low[a, :, :PANELS]), NN)
        pair_out[pair] = dot3(halves(part), split[e], NT)


def whole(shape):
    return pl.BlockSpec(shape, lambda *_: (0,) * len(shape))


def fit_call(ids, near, count, window, skeleton, blocks):
    return pl.pallas_call(
        fit_kernel,
        grid_spec=pltpu.PrefetchScalarGridSpec(
            num_scalar_prefetch=3,
            grid=(1,),
            in_specs=[
                whole((3 * BOXES, 4, PANELS)),
                whole((BOXES, SLOTS)),
                pl.BlockSpec((MINE, PANELS, PANELS), lambda i, ids, *_: (ids[1], 0, 0)),
            ],
            out_specs=[
                whole((MINE, SLOTS, PANELS)),
                whole((MINE, SLOTS, NEAR * PANELS)),
                whole((MINE, SLOTS, SLOTS)),
                whole((MINE // 2, SLOTS, SLOTS)),
            ],
            scratch_shapes=[
                pltpu.VMEM((MINE, 3, PANELS, SLOTS), F32),
                pltpu.VMEM((MINE, PANELS, NEAR * PANELS), BF16),
                pltpu.VMEM((MINE, PANELS, NEAR * PANELS), BF16),
                pltpu.VMEM((MINE, PANELS, PANELS), F32),
            ],
        ),
        out_shape=[
            jax.ShapeDtypeStruct((MINE, SLOTS, PANELS), F32),
            jax.ShapeDtypeStruct((MINE, SLOTS, NEAR * PANELS), F32),
            jax.ShapeDtypeStruct((MINE, SLOTS, SLOTS), F32),
            jax.ShapeDtypeStruct((MINE // 2, SLOTS, SLOTS), F32),
        ],
        compiler_params=pltpu.CompilerParams(vmem_limit_bytes=56 * MIB),
        name="fit",
    )(ids, near, count, window, skeleton, blocks)


def exchange_kernel(
    skeleton, owners, counts, fits, window, table,
    mine, via, own_sem, send_sem, recv_sem, pass_sem, take_sem, line_send, line_recv, plane_send, plane_recv,
):
    home, member = place()
    side_hi, core = member // 2, lax.rem(member, 2)
    side_lo = lax.rem(home, 2)
    sign = 1 - 2 * side_hi
    outer = side_lo == side_hi
    flipped = home + 1 - 2 * side_lo
    side = (flipped, member)
    cross = (flipped, 2 * (1 - side_hi) + core)
    above = (lax.rem(home + 2 * sign + HOMES, HOMES), member)
    below = (lax.rem(home - 2 * sign + HOMES, HOMES), member)
    sibling = (home, 2 * side_hi + 1 - core)
    line, plane, across, along = lines_of(home, member)
    enter([side, cross, above, below, sibling] + line + [peer for _, peer in plane])

    def slot(shift, k, to=1):
        return window.at[2 * (2 + to * sign * shift) + core, k]

    def moved(source, target, stream, k, peer, recv):
        return send(source, target, send_sem.at[stream, k], recv_sem.at[recv, k], peer)

    def passed(source, shift, i, k):
        return send(source, slot(shift, k), pass_sem.at[i, k], take_sem.at[i, k], sibling)

    boxes = range(MINE)
    own = pltpu.make_async_copy(fits, window.at[4 + core], own_sem.at[0])

    lane = lax.broadcasted_iota(jnp.int32, (1, SLOTS), 1)
    owner_row = jnp.zeros((1, SLOTS), jnp.int32)
    count_row = jnp.zeros((1, SLOTS), jnp.int32)
    for s in range(8):
        owner_row = jnp.where(lane == s, owners[s], owner_row)
        count_row = jnp.where(lane == s, counts[s], count_row)
    mine[0:8, :] = skeleton[...]
    mine[8:16, :] = jnp.zeros((8, SLOTS), jnp.int32)
    mine[8:9, :] = owner_row
    mine[9:10, :] = count_row

    def own_streams(first_peer, first_target, second_peer, second_target, second_recv):
        copies = []
        for k in boxes:
            copies.append(moved(fits.at[k], first_target(k), 0, k, first_peer, 0))
            copies.append(moved(fits.at[k], second_target(k), 1, k, second_peer, second_recv))
            copies.append(passed(fits.at[k], 0, 4, k))
        for copy in copies:
            copy.start()
        own.start()
        return copies

    def arrival(shift, stream, k):
        return moved(slot(shift, k), slot(shift, k), stream, k, side, stream)

    def gather_line():
        spot = table.at[across, along]
        placed = pltpu.make_async_copy(mine, spot, own_sem.at[1])
        placed.start()
        copies = [send(mine, spot, line_send.at[i], line_recv.at[i], peer) for i, peer in enumerate(line)]
        for copy in copies:
            copy.start()
        placed.wait()
        return copies

    def gather_plane():
        copies = [
            send(table.at[across], table.at[across], plane_send.at[i], plane_recv.at[i], peer)
            for i, (_, peer) in enumerate(plane)
        ]
        for copy in copies:
            copy.start()
        return copies

    def finish(copies, gathers):
        for copy in copies + gathers:
            copy.wait_send()
        for i in range(5):
            for k in boxes:
                passed(fits.at[k], 0, i, k).wait_recv()
        own.wait()

    def start(copies, *new):
        for copy in new:
            copy.start()
            copies.append(copy)

    @pl.when(outer)
    def _():
        copies = own_streams(
            side, lambda k: slot(-2, k), below, lambda k: via.at[k], 1
        )
        gathers = gather_line()
        planes = []
        for k in range(MINE + 1):
            if k < MINE:
                arrival(2, 0, k).wait_recv()
                start(copies, moved(slot(2, k), slot(-2, k), 2, k, above, 2))
                if k % 2:
                    start(copies, moved(slot(2, k), slot(1, k, -1), 4, k, cross, 4))
                start(copies, passed(slot(2, k), 2, 0, k))
                moved(via.at[k], via.at[k], 1, k, side, 1).wait_recv()
                start(copies, moved(via.at[k], slot(-1, k, -1), 3, k, cross, 3))
            if k == 1:
                for copy in gathers:
                    copy.wait_recv()
                planes = gather_plane()
            if k:
                arrival(-2, 2, k - 1).wait_recv()
                start(copies, passed(slot(-2, k - 1), -2, 1, k - 1))
                arrival(-1, 3, k - 1).wait_recv()
                start(copies, passed(slot(-1, k - 1), -1, 2, k - 1))
                arrival(1, 4, k - 1).wait_recv()
                start(copies, passed(slot(1, k - 1), 1, 3, k - 1))
        for copy in planes:
            copy.wait_recv()
        finish(copies, gathers + planes)

    @pl.when(jnp.logical_not(outer))
    def _():
        copies = own_streams(
            side, lambda k: slot(2, k), cross, lambda k: slot(-1, k, -1), 1
        )
        gathers = gather_line()
        planes = []
        for k in range(MINE + 1):
            if k < MINE:
                arrival(-2, 0, k).wait_recv()
                start(copies, moved(slot(-2, k), slot(1, k, -1), 2, k, cross, 2))
                start(copies, moved(slot(-2, k), slot(2, k), 3, k, below, 3))
                start(copies, passed(slot(-2, k), -2, 0, k))
                arrival(-1, 1, k).wait_recv()
                if k % 2 == 0:
                    start(copies, moved(slot(-1, k), slot(1, k), 4, k, side, 4))
                start(copies, passed(slot(-1, k), -1, 1, k))
            if k == 1:
                for copy in gathers:
                    copy.wait_recv()
                planes = gather_plane()
            if k:
                arrival(1, 2, k - 1).wait_recv()
                start(copies, passed(slot(1, k - 1), 1, 2, k - 1))
                arrival(2, 3, k - 1).wait_recv()
                start(copies, passed(slot(2, k - 1), 2, 3, k - 1))
        for copy in planes:
            copy.wait_recv()
        finish(copies, gathers + planes)


def exchange(skeleton, owners, counts, fits):
    dma = pltpu.SemaphoreType.DMA
    return pl.pallas_call(
        exchange_kernel,
        out_shape=[
            jax.ShapeDtypeStruct((10, MINE, SLOTS, PANELS), F32),
            jax.ShapeDtypeStruct((W, Z, 16, SLOTS), jnp.int32),
        ],
        in_specs=[
            pl.BlockSpec(memory_space=pltpu.VMEM),
            pl.BlockSpec(memory_space=pltpu.SMEM),
            pl.BlockSpec(memory_space=pltpu.SMEM),
            pl.BlockSpec(memory_space=pl.ANY),
        ],
        out_specs=[pl.BlockSpec(memory_space=pl.ANY)] * 2,
        scratch_shapes=[
            pltpu.VMEM((16, SLOTS), jnp.int32),
            pltpu.VMEM((MINE, SLOTS, PANELS), F32),
            dma((2,)), dma((5, MINE)), dma((5, MINE)), dma((5, MINE)), dma((5, MINE)),
            dma((Z - 1,)), dma((Z - 1,)), dma((W - 1,)), dma((W - 1,)),
        ],
        compiler_params=pltpu.CompilerParams(collective_id=1, has_side_effects=True),
        name="exchange",
    )(skeleton, owners, counts, fits)


def level_kernel(ids, near, fitw, left, block, pair, table, one_out, two_out, high, low, merged):
    home, member = ids[0], ids[1]
    first = member * MINE
    base = 16 * home + 8 * (member // 2) - 16

    for own in range(MINE):
        for index in range(NEAR):
            box = near[first + own, index] - base
            lanes = slice(index * PANELS, (index + 1) * PANELS)
            hi, lo = halves(dot3(halves(left[own, :, lanes]), halves(fitw[box]), NT))
            high[own, :, index * SLOTS : (index + 1) * SLOTS] = hi
            low[own, :, index * SLOTS : (index + 1) * SLOTS] = lo
        one_out[own] = block[own] - square((high[own], low[own]), NT)
    grams, rights, picks, bodies = [], [], [], []
    for j in range(MINE // 2):
        cross = pair[j]
        merged[j, :SLOTS, :SLOTS] = one_out[2 * j]
        merged[j, :SLOTS, SLOTS:] = cross
        merged[j, SLOTS:, :SLOTS] = cross.T
        merged[j, SLOTS:, SLOTS:] = one_out[2 * j + 1]
        body = halves(merged[j])
        parent = (home * BOXES + first) // 2 + j
        spot = lax.broadcasted_iota(jnp.int32, (W * Z, SLOTS), 0)
        lane = lax.broadcasted_iota(jnp.int32, (W * Z, SLOTS), 1)
        found = (table[:, 8, :] == parent) & (lane < 8)
        slot = jnp.sum(jnp.where(found, (8 * spot + lane).astype(F32), 0.0)).astype(jnp.int32)
        spot, slot = slot // 8, lax.rem(slot, 8)
        lane = lax.broadcasted_iota(jnp.int32, (1, SLOTS), 1)
        count = jnp.sum(jnp.where(lane == slot, table[spot, 9:10, :].astype(F32), 0.0)).astype(jnp.int32)
        columns = chosen_columns(table[spot, pl.ds(slot, 1), :], count)
        gram, right, pick = normal(square(body, TN), columns)
        grams.append(gram)
        rights.append(right)
        picks.append(pick)
        bodies.append(body)
    fits = refine(grams, rights, picks)
    for j in range(MINE // 2):
        fit = halves(fits[j])
        two_out[j] = dot3(halves(dot3(fit, bodies[j], NN)), fit, NT)


def level_call(ids, near, fitw, left, block, pair, table):
    return pl.pallas_call(
        level_kernel,
        grid_spec=pltpu.PrefetchScalarGridSpec(
            num_scalar_prefetch=2,
            grid=(1,),
            in_specs=[
                whole(fitw.shape),
                whole(left.shape),
                whole(block.shape),
                whole(pair.shape),
                whole(table.shape),
            ],
            out_specs=[whole((MINE, SLOTS, SLOTS)), whole((MINE // 2, SLOTS, SLOTS))],
            scratch_shapes=[
                pltpu.VMEM((MINE, SLOTS, NEAR * SLOTS), BF16),
                pltpu.VMEM((MINE, SLOTS, NEAR * SLOTS), BF16),
                pltpu.VMEM((MINE // 2, PANELS, PANELS), F32),
            ],
        ),
        out_shape=[
            jax.ShapeDtypeStruct((MINE, SLOTS, SLOTS), F32),
            jax.ShapeDtypeStruct((MINE // 2, SLOTS, SLOTS), F32),
        ],
        compiler_params=pltpu.CompilerParams(vmem_limit_bytes=56 * MIB),
        name="level",
    )(ids, near, fitw, left, block, pair, table)


def route_kernel(
    table, one, two, one_out, two_out, owners, lines0, lines1, packed, arrived0, arrived1,
    own_sem, row_send, row_recv, block_send, block_recv, up_send, up_recv, down_send, down_recv, plane_send, plane_recv,
):
    home, member = place()
    line, plane, across, along = lines_of(home, member)
    up, down = line[0], line[-1]
    members = [(home, lax.rem(member + d, MEMBERS)) for d in range(1, MEMBERS)]
    listing = pltpu.make_async_copy(table.at[:, 8], owners, own_sem.at[2])
    listing.start()
    enter(members + [up, down] + [peer for _, peer in plane])
    half = ROWS // PARTS
    lines, arrived = (lines0, lines1), (arrived0, arrived1)

    def rows(array, target, part=None):
        first, count = (target * ROWS, ROWS) if part is None else (target * ROWS + part * half, half)
        return array.at[:, pl.ds(pl.multiple_of(first, half), count), :]

    def ours(part):
        return lines[part].at[along, pl.ds(2 * member, 2)]

    own_two = [
        pltpu.make_async_copy(rows(two, member, part), ours(part), own_sem.at[3 + part]) for part in range(PARTS)
    ]
    own_one = pltpu.make_async_copy(rows(one, member), one_out.at[pl.ds(MINE * member, MINE)], own_sem.at[0])
    blocks = [
        [
            send(rows(two, peer[1], part), ours(part), block_send.at[part, i], block_recv.at[part, i], peer)
            for i, peer in enumerate(members)
        ]
        for part in range(PARTS)
    ]
    ones = [
        send(rows(one, peer[1]), one_out.at[pl.ds(MINE * member, MINE)], row_send.at[i], row_recv.at[i], peer)
        for i, peer in enumerate(members)
    ]
    for part in range(PARTS):
        for copy in blocks[part]:
            copy.start()
        own_two[part].start()
    for copy in ones:
        copy.start()
    own_one.start()

    def upward(part, step):
        spot = lines[part].at[lax.rem(along - step + Z, Z)]
        return send(spot, spot, up_send.at[part, step], up_recv.at[part, step], up)

    def downward(part, step):
        spot = lines[part].at[lax.rem(along + step, Z)]
        return send(spot, spot, down_send.at[part, step], down_recv.at[part, step], down)

    def steps(part):
        return (4, 3) if part % 2 == 0 else (3, 4)

    def gather(part, step):
        for way, copy in enumerate((upward, downward)):
            if step and step - 1 < steps(part)[way]:
                copy(part, step - 1).wait_recv()
            if step < steps(part)[way]:
                copy(part, step).start()

    def pack(target, at):
        spot = 8 * at + along
        for s in range(8):
            parent = owners[spot, s]
            source = parent // 8
            target(s, lax.rem(source // 2, Z), lax.rem(parent, 8))

    def across_copy(part, i):
        return send(
            packed.at[part, i], arrived[part].at[across], plane_send.at[part, i], plane_recv.at[part, i], plane[i][1]
        )

    def send_across(part):
        for i, (spot, _) in enumerate(plane):

            def put(s, z, j):
                packed[part, i, s] = lines[part][z, j]

            pack(put, spot)
            across_copy(part, i).start()

        def put(s, z, j):
            arrived[part][across, s] = lines[part][z, j]

        pack(put, across)

    for part in range(PARTS):
        own_two[part].wait()
        for copy in blocks[part]:
            copy.wait_recv()
        gather(part, 0)
    listing.wait()
    for step in range(1, 6):
        if step < 5:
            gather(0, step)
        if step > 1:
            gather(1, step - 1)
        if step > 3:
            send_across(step - 4)
    spot = 8 * across + along
    for part in range(PARTS):
        for i in range(W - 1):
            across_copy(part, i).wait_recv()
        for s in range(8):
            source = owners[spot, s] // 8
            two_out[s, part * half : (part + 1) * half, :] = arrived[part][2 * (source // 16) + lax.rem(source, 2), s]
    own_one.wait()
    for copy in ones:
        copy.wait()
    for part in range(PARTS):
        for copy in blocks[part]:
            copy.wait_send()
        for step in range(4):
            for way, copy in enumerate((upward, downward)):
                if step < steps(part)[way]:
                    copy(part, step).wait_send()
        for i in range(W - 1):
            across_copy(part, i).wait_send()


def route(table, one, two):
    dma = pltpu.SemaphoreType.DMA
    half = ROWS // PARTS
    return pl.pallas_call(
        route_kernel,
        out_shape=[
            jax.ShapeDtypeStruct((BOXES, ROWS, SLOTS), F32),
            jax.ShapeDtypeStruct((8, ROWS, SLOTS), F32),
        ],
        in_specs=[pl.BlockSpec(memory_space=pl.ANY)] * 3,
        out_specs=[pl.BlockSpec(memory_space=pl.ANY), pl.BlockSpec(memory_space=pltpu.VMEM)],
        scratch_shapes=[
            pltpu.SMEM((W * Z, SLOTS), jnp.int32),
            pltpu.VMEM((Z, 8, half, SLOTS), F32),
            pltpu.VMEM((Z, 8, half, SLOTS), F32),
            pltpu.VMEM((PARTS, W - 1, 8, half, SLOTS), F32),
            pltpu.VMEM((W, 8, half, SLOTS), F32),
            pltpu.VMEM((W, 8, half, SLOTS), F32),
            dma((3 + PARTS,)), dma((3,)), dma((3,)), dma((PARTS, 3)), dma((PARTS, 3)),
            dma((PARTS, 4)), dma((PARTS, 4)), dma((PARTS, 4)), dma((PARTS, 4)),
            dma((PARTS, W - 1)), dma((PARTS, W - 1)),
        ],
        compiler_params=pltpu.CompilerParams(collective_id=2, has_side_effects=True),
        name="route",
    )(table, one, two)


def local(panels, self_blocks, neighbors, skeleton_one, count_one, skeleton_two, count_two, parent_at_slot):
    home, member = place()
    ids = jnp.stack([home, member]).astype(jnp.int32)
    window = halo(panels)
    fitw, left, block, pair = fit_call(ids, neighbors, count_one, window, skeleton_one, self_blocks)
    reach, table = exchange(skeleton_two, parent_at_slot, count_two, fitw)
    reach, table = reach.reshape(10 * MINE, SLOTS, PANELS), table.reshape(W * Z, 16, SLOTS)
    one, two = level_call(ids, neighbors, reach, left, block, pair, table)
    return route(table, one, two)


def solution(mesh):
    placed = (
        P("box", None, None),
        P("box", None, None),
        P("box", None),
        P("box", None),
        P("box"),
        P("box", None),
        P("box"),
        P("box"),
    )
    return jax.shard_map(
        local,
        mesh=mesh,
        in_specs=placed,
        out_specs=(P("box", "blk", None), P("box", "blk", None)),
        check_vma=False,
    )
```

```python
import jax
import jax.numpy as jnp
from jax import lax
from jax.experimental import pallas as pl
from jax.experimental.pallas import tpu as pltpu
from jax.sharding import PartitionSpec as P

STEPS = 3
MESH = pl.DeviceIdType.MESH
F32 = jnp.float32
BF16 = jnp.bfloat16
NN = (((1,), (0,)), ((), ()))
NT = (((1,), (1,)), ((), ()))
TN = (((0,), (0,)), ((), ()))
MIB = 1 << 20

HOMES, MEMBERS = 64, 4
BOXES, MINE = 16, 4
PANELS, SLOTS, NEAR = 256, 128, 8
Z, W = 8, 8
ROWS = SLOTS // MEMBERS
PARTS = 2


def halves(x):
    high = x.astype(BF16)
    return high, (x - high.astype(F32)).astype(BF16)


def dot(a, b, dims):
    return lax.dot_general(a, b, dims, preferred_element_type=F32)


def dot3(a, b, dims):
    return dot(a[0], b[0], dims) + (dot(a[0], b[1], dims) + dot(a[1], b[0], dims))


def square(a, dims):
    cross = dot(a[0], a[1], dims)
    return dot(a[0], a[0], dims) + (cross + cross.T)


def within(index, count):
    return jnp.minimum(jnp.maximum(index, 0), count - 1)


def place():
    home, member = lax.axis_index("box"), lax.axis_index("blk")
    return home, member


def enter(peers):
    barrier = pltpu.get_barrier_semaphore()
    for peer in peers:
        pl.semaphore_signal(barrier, inc=1, device_id=peer, device_id_type=MESH)
    pl.semaphore_wait(barrier, len(peers))


def send(source, target, send_sem, recv_sem, peer):
    return pltpu.make_async_remote_copy(
        src_ref=source,
        dst_ref=target,
        send_sem=send_sem,
        recv_sem=recv_sem,
        device_id=peer,
        device_id_type=MESH,
    )


def home_at(across, along):
    return (across // 2) * 16 + along * 2 + lax.rem(across, 2)


def lines_of(home, member):
    across = 2 * (home // 16) + lax.rem(home, 2)
    along = lax.rem(home // 2, Z)
    line = [(home_at(across, lax.rem(along + d, Z)), member) for d in range(1, Z)]
    spots = [lax.rem(across + d, W) for d in range(1, W)]
    plane = [(spot, (home_at(spot, along), member)) for spot in spots]
    return line, plane, across, along


def refine(gram, right, chosen):
    steps = [1.0 / jnp.max(jnp.sum(jnp.abs(g), axis=1, keepdims=True), axis=0, keepdims=True) for g in gram]
    grams = [halves(g) for g in gram]
    fits = list(chosen)
    for _ in range(STEPS):
        updates = [r - dot3(g, halves(f), NN) for g, r, f in zip(grams, right, fits)]
        fits = [f + s * u for f, s, u in zip(fits, steps, updates)]
    return fits


def chosen_columns(row, count):
    position = lax.broadcasted_iota(jnp.int32, (2 * SLOTS, SLOTS), 0)
    slot = lax.broadcasted_iota(jnp.int32, (2 * SLOTS, SLOTS), 1)
    return jnp.where((position == row) & (slot < count), 1.0, 0.0).astype(F32)


def normal(square_matrix, columns):
    picks = columns.T
    picks16 = picks.astype(BF16)
    columns16 = columns.astype(BF16)
    high, low = halves(square_matrix)
    right = dot(picks16, high, NN) + dot(picks16, low, NN)
    high, low = halves(right)
    gram = dot(high, columns16, NN) + dot(low, columns16, NN)
    return gram, right, picks


def couple(col, row):
    total = None
    for axis in range(3):
        offset = col[axis] - row[axis]
        total = offset * offset if total is None else total + offset * offset
    return 0.03125 * lax.rsqrt(total + 0.01)


SCRATCH = [
    ("window", (3 * BOXES, 4, PANELS), F32),
    ("column", (3, PANELS, SLOTS), F32),
    ("high", (MINE, PANELS, NEAR * PANELS), BF16),
    ("low", (MINE, PANELS, NEAR * PANELS), BF16),
    ("fit_high", (MINE, SLOTS, PANELS), BF16),
    ("fit_low", (MINE, SLOTS, PANELS), BF16),
    ("left_high", (MINE, SLOTS, NEAR * PANELS), BF16),
    ("left_low", (MINE, SLOTS, NEAR * PANELS), BF16),
    ("reach", (10 * MINE, SLOTS, PANELS), F32),
    ("via", (MINE, SLOTS, PANELS), F32),
    ("blocks", (MINE, PANELS, PANELS), F32),
    ("block", (MINE, SLOTS, SLOTS), F32),
    ("pair", (MINE // 2, SLOTS, SLOTS), F32),
    ("cross_high", (SLOTS, NEAR * SLOTS), BF16),
    ("cross_low", (SLOTS, NEAR * SLOTS), BF16),
    ("one", (MINE, SLOTS, SLOTS), F32),
    ("merged", (MINE // 2, PANELS, PANELS), F32),
    ("two", (MINE // 2, SLOTS, SLOTS), F32),
    ("mine", (16, SLOTS), jnp.int32),
    ("table", (W, Z, 16, SLOTS), jnp.int32),
    ("lines0", (Z, 8, ROWS // PARTS, SLOTS), F32),
    ("lines1", (Z, 8, ROWS // PARTS, SLOTS), F32),
    ("packed", (PARTS, W - 1, 8, ROWS // PARTS, SLOTS), F32),
    ("arrived0", (W, 8, ROWS // PARTS, SLOTS), F32),
    ("arrived1", (W, 8, ROWS // PARTS, SLOTS), F32),
]
COPIES = [
    ("own", (8,)),
    ("halo_send", (2,)), ("halo_recv", (2,)),
    ("send", (5, MINE)), ("recv", (5, MINE)), ("give", (5, MINE)), ("take", (5, MINE)),
    ("table_line_send", (Z - 1,)), ("table_line_recv", (Z - 1,)),
    ("table_plane_send", (W - 1,)), ("table_plane_recv", (W - 1,)),
    ("row_send", (3,)), ("row_recv", (3,)), ("block_send", (PARTS, 3)), ("block_recv", (PARTS, 3)),
    ("up_send", (PARTS, 4)), ("up_recv", (PARTS, 4)), ("down_send", (PARTS, 4)), ("down_recv", (PARTS, 4)),
    ("plane_send", (PARTS, W - 1)), ("plane_recv", (PARTS, W - 1)),
]


class Refs:
    def __init__(self, refs):
        names = ["near", "owners"] + [name for name, *_ in SCRATCH] + [name + "_sem" for name, _ in COPIES]
        for name, ref in zip(names, refs, strict=True):
            setattr(self, name, ref)


def kernel(
    panels, self_blocks, neighbors, skeleton_one, count_one, skeleton_two, count_two, parent_at_slot, one_out, two_out, *refs
):
    v = Refs(refs)
    home, member = place()
    first = member * MINE
    boxes = range(MINE)
    side_hi, core = member // 2, lax.rem(member, 2)
    side_lo = lax.rem(home, 2)
    sign = 1 - 2 * side_hi
    outer = side_lo == side_hi
    flipped = home + 1 - 2 * side_lo
    side = (flipped, member)
    cross = (flipped, 2 * (1 - side_hi) + core)
    above = (lax.rem(home + 2 * sign + HOMES, HOMES), member)
    below = (lax.rem(home - 2 * sign + HOMES, HOMES), member)
    after = (lax.rem(home + 1, HOMES), member)
    before = (lax.rem(home + HOMES - 1, HOMES), member)
    sibling = (home, 2 * side_hi + 1 - core)
    members = [(home, lax.rem(member + d, MEMBERS)) for d in range(1, MEMBERS)]
    line, plane, across, along = lines_of(home, member)

    stage_near = pltpu.make_async_copy(neighbors, v.near, v.own_sem.at[0])
    stage_blocks = pltpu.make_async_copy(self_blocks.at[pl.ds(first, MINE)], v.blocks, v.own_sem.at[1])
    stage_panels = pltpu.make_async_copy(panels, v.window.at[pl.ds(BOXES, BOXES)], v.own_sem.at[2])
    stage_near.start()
    stage_panels.start()
    stage_blocks.start()

    lane = lax.broadcasted_iota(jnp.int32, (1, SLOTS), 1)
    owner_row = jnp.zeros((1, SLOTS), jnp.int32)
    count_row = jnp.zeros((1, SLOTS), jnp.int32)
    for s in range(8):
        owner_row = jnp.where(lane == s, parent_at_slot[s], owner_row)
        count_row = jnp.where(lane == s, count_two[s], count_row)
    v.mine[0:8, :] = skeleton_two[...]
    v.mine[8:16, :] = jnp.zeros((8, SLOTS), jnp.int32)
    v.mine[8:9, :] = owner_row
    v.mine[9:10, :] = count_row

    enter([after, before, cross, above, below] + members + line + [peer for _, peer in plane])

    halos = [
        send(panels, v.window.at[pl.ds(0, BOXES)], v.halo_send_sem.at[0], v.halo_recv_sem.at[0], after),
        send(panels, v.window.at[pl.ds(2 * BOXES, BOXES)], v.halo_send_sem.at[1], v.halo_recv_sem.at[1], before),
    ]
    for copy in halos:
        copy.start()

    spot = v.table.at[across, along]
    stage_table = pltpu.make_async_copy(v.mine, spot, v.own_sem.at[3])
    stage_table.start()
    table_line = [
        send(v.mine, spot, v.table_line_send_sem.at[i], v.table_line_recv_sem.at[i], peer) for i, peer in enumerate(line)
    ]
    for copy in table_line:
        copy.start()
    table_plane = [
        send(v.table.at[across], v.table.at[across], v.table_plane_send_sem.at[i], v.table_plane_recv_sem.at[i], peer)
        for i, (_, peer) in enumerate(plane)
    ]

    def slot(shift, k, to=1):
        return v.reach.at[MINE * (2 * (2 + to * sign * shift) + core) + k]

    def moved(source, target, stream, k, peer, recv):
        return send(source, target, v.send_sem.at[stream, k], v.recv_sem.at[recv, k], peer)

    def passed(shift, i, k):
        return send(slot(shift, k), slot(shift, k), v.give_sem.at[i, k], v.take_sem.at[i, k], sibling)

    def arrival(stream, k):
        return moved(slot(0, k), slot(0, k), stream, k, side, stream)

    def at_outer(body):
        pl.when(outer)(body)

    def at_inner(body):
        pl.when(jnp.logical_not(outer))(body)

    def outer_moves(k):
        return {
            "own": [
                moved(slot(0, k), slot(-2, k), 0, k, side, 0),
                moved(slot(0, k), v.via.at[k], 1, k, below, 1),
            ],
            "side": [moved(slot(2, k), slot(-2, k), 2, k, above, 2)]
            + ([moved(slot(2, k), slot(1, k, -1), 4, k, cross, 4)] if k % 2 else []),
            "next": [moved(v.via.at[k], slot(-1, k, -1), 3, k, cross, 3)],
        }

    def inner_moves(k):
        return {
            "own": [
                moved(slot(0, k), slot(2, k), 0, k, side, 0),
                moved(slot(0, k), slot(-1, k, -1), 1, k, cross, 1),
            ],
            "side": [
                moved(slot(-2, k), slot(1, k, -1), 2, k, cross, 2),
                moved(slot(-2, k), slot(2, k), 3, k, below, 3),
            ],
            "next": [moved(slot(-1, k), slot(1, k), 4, k, side, 4)] if k % 2 == 0 else [],
        }

    def begin(copies):
        for copy in copies:
            copy.start()

    def send_own(k):
        at_outer(lambda: begin(outer_moves(k)["own"]))
        at_inner(lambda: begin(inner_moves(k)["own"]))
        passed(0, 4, k).start()

    def early(k):
        @at_outer
        def _():
            arrival(0, k).wait_recv()
            begin(outer_moves(k)["side"] + [passed(2, 0, k)])
            arrival(1, k).wait_recv()
            begin(outer_moves(k)["next"])

        @at_inner
        def _():
            arrival(0, k).wait_recv()
            begin(inner_moves(k)["side"] + [passed(-2, 0, k)])
            arrival(1, k).wait_recv()
            begin(inner_moves(k)["next"] + [passed(-1, 1, k)])

    def late(k):
        @at_outer
        def _():
            for stream, shift, i in ((2, -2, 1), (3, -1, 2), (4, 1, 3)):
                arrival(stream, k).wait_recv()
                passed(shift, i, k).start()

        @at_inner
        def _():
            for stream, shift, i in ((2, 1, 2), (3, 2, 3)):
                arrival(stream, k).wait_recv()
                passed(shift, i, k).start()

    def taken():
        for k in boxes:
            for i in range(5):
                passed(0, i, k).wait_recv()

    def sent():
        for k in boxes:

            @at_outer
            def _():
                for copies in outer_moves(k).values():
                    for copy in copies:
                        copy.wait_send()

            @at_inner
            def _():
                for copies in inner_moves(k).values():
                    for copy in copies:
                        copy.wait_send()

            for i in range(5):
                passed(0, i, k).wait_send()

    tile = 64

    def couple_with(box, write):
        for part in range(PANELS // SLOTS):
            lanes = slice(part * SLOTS, (part + 1) * SLOTS)
            row = [v.window[box, axis : axis + 1, lanes] for axis in range(3)]
            for start in range(0, PANELS, tile):
                col = [v.column[axis, start : start + tile, :] for axis in range(3)]
                hi, lo = halves(couple(col, row))
                write(start, part, hi, lo)

    def columns_of(own):
        for axis in range(3):
            row = v.window[BOXES + first + own, axis : axis + 1, :]
            v.column[axis] = jnp.broadcast_to(row, (SLOTS, PANELS)).T

    def split_fit(own):
        return v.fit_high[own], v.fit_low[own]

    def fit_box(own):
        columns_of(own)

        def proxy(index, carry):
            box = within(v.near[first + own, index] - (home - 1) * BOXES, 3 * BOXES)

            def write(start, part, hi, lo):
                lanes = pl.ds(pl.multiple_of(index * PANELS + part * SLOTS, SLOTS), SLOTS)
                v.high[own, start : start + tile, lanes] = hi
                v.low[own, start : start + tile, lanes] = lo

            couple_with(box, write)
            return carry

        lax.fori_loop(0, NEAR, proxy, 0)
        columns = chosen_columns(skeleton_one[pl.ds(first + own, 1), :], count_one[first + own])
        gram, right, pick = normal(square((v.high[own], v.low[own]), NT), columns)
        (fit,) = refine([gram], [right], [pick])
        weight = jnp.sum(fit * fit * v.window[BOXES + first + own, 3:4, :], axis=1, keepdims=True)
        v.reach[MINE * (4 + core) + own] = fit * lax.rsqrt(jnp.maximum(weight, 1.0))
        v.fit_high[own], v.fit_low[own] = halves(fit)

    def left_box(own):
        for index in range(NEAR):
            lanes = slice(index * PANELS, (index + 1) * PANELS)
            product = dot3(split_fit(own), (v.high[own, :, lanes], v.low[own, :, lanes]), NN)
            v.left_high[own, :, lanes], v.left_low[own, :, lanes] = halves(product)
        part = dot3(split_fit(own), halves(v.blocks[own]), NN)
        v.block[own] = dot3(halves(part), split_fit(own), NT)

    def pair_of(j):
        a, e = 2 * j, 2 * j + 1
        columns_of(a)

        def write(start, part, hi, lo):
            lanes = slice(part * SLOTS, (part + 1) * SLOTS)
            v.high[a, start : start + tile, lanes] = hi
            v.low[a, start : start + tile, lanes] = lo

        couple_with(BOXES + first + e, write)
        part = dot3(split_fit(a), (v.high[a, :, :PANELS], v.low[a, :, :PANELS]), NN)
        v.pair[j] = dot3(halves(part), split_fit(e), NT)

    stage_near.wait()
    stage_panels.wait()
    for copy in halos:
        copy.wait_recv()
    fit_box(0)
    send_own(0)
    fit_box(1)
    send_own(1)
    early(0)
    for copy in table_line:
        copy.wait_recv()
    stage_table.wait()
    begin(table_plane)
    fit_box(2)
    send_own(2)
    early(1)
    late(0)
    fit_box(3)
    send_own(3)
    early(2)
    late(1)
    stage_blocks.wait()
    left_box(0)
    left_box(1)
    early(3)
    late(2)
    pair_of(0)
    left_box(2)
    left_box(3)
    pair_of(1)
    late(3)
    for copy in table_plane:
        copy.wait_recv()
    listing = pltpu.make_async_copy(v.table.at[:, :, 8], v.owners, v.own_sem.at[4])
    listing.start()
    taken()

    base = 16 * home + 8 * side_hi - 16
    for own in boxes:
        for index in range(NEAR):
            box = within(v.near[first + own, index] - base, 10 * MINE)
            lanes = slice(index * PANELS, (index + 1) * PANELS)
            left = (v.left_high[own, :, lanes], v.left_low[own, :, lanes])
            lanes = slice(index * SLOTS, (index + 1) * SLOTS)
            v.cross_high[:, lanes], v.cross_low[:, lanes] = halves(dot3(left, halves(v.reach[box]), NT))
        v.one[own] = v.block[own] - square((v.cross_high[...], v.cross_low[...]), NT)

    def rows(array, target, first_row, count):
        return array.at[:, pl.ds(pl.multiple_of(target * ROWS + first_row, count), count), :]

    mine_one = one_out.at[pl.ds(MINE * member, MINE)]
    own_one = pltpu.make_async_copy(rows(v.one, member, 0, ROWS), mine_one, v.own_sem.at[5])
    ones = [
        send(rows(v.one, peer[1], 0, ROWS), mine_one, v.row_send_sem.at[i], v.row_recv_sem.at[i], peer)
        for i, peer in enumerate(members)
    ]
    begin(ones + [own_one])

    grams, rights, picks, bodies = [], [], [], []
    for j in range(MINE // 2):
        between = v.pair[j]
        v.merged[j, :SLOTS, :SLOTS] = v.one[2 * j]
        v.merged[j, :SLOTS, SLOTS:] = between
        v.merged[j, SLOTS:, :SLOTS] = between.T
        v.merged[j, SLOTS:, SLOTS:] = v.one[2 * j + 1]
        body = halves(v.merged[j])
        parent = (home * BOXES + first) // 2 + j
        lane = lax.broadcasted_iota(jnp.int32, (W * Z, SLOTS), 1)
        table = v.table.reshape(W * Z, 16, SLOTS)
        found = ((table[:, 8, :] == parent) & (lane < 8)).astype(F32)
        row = jnp.zeros((1, SLOTS), F32)
        for s in range(8):
            row = row + jnp.sum(found[:, s : s + 1] * table[:, s, :].astype(F32), axis=0, keepdims=True)
        count = jnp.sum(jnp.sum(found * table[:, 9, :].astype(F32), axis=0, keepdims=True), axis=1, keepdims=True)
        columns = chosen_columns(row.astype(jnp.int32), count.astype(jnp.int32))
        gram, right, pick = normal(square(body, TN), columns)
        grams.append(gram)
        rights.append(right)
        picks.append(pick)
        bodies.append(body)
    fits = refine(grams, rights, picks)
    for j in range(MINE // 2):
        fit = halves(fits[j])
        v.two[j] = dot3(halves(dot3(fit, bodies[j], NN)), fit, NT)

    up, down = line[0], line[-1]
    half = ROWS // PARTS
    lines, arrived = (v.lines0, v.lines1), (v.arrived0, v.arrived1)

    def ours(part):
        return lines[part].at[along, pl.ds(2 * member, 2)]

    own_two = [
        pltpu.make_async_copy(rows(v.two, member, part * half, half), ours(part), v.own_sem.at[6 + part])
        for part in range(PARTS)
    ]
    parts = [
        [
            send(
                rows(v.two, peer[1], part * half, half),
                ours(part),
                v.block_send_sem.at[part, i],
                v.block_recv_sem.at[part, i],
                peer,
            )
            for i, peer in enumerate(members)
        ]
        for part in range(PARTS)
    ]
    for part in range(PARTS):
        begin(parts[part] + [own_two[part]])

    def upward(part, step):
        spot = lines[part].at[lax.rem(along - step + Z, Z)]
        return send(spot, spot, v.up_send_sem.at[part, step], v.up_recv_sem.at[part, step], up)

    def downward(part, step):
        spot = lines[part].at[lax.rem(along + step, Z)]
        return send(spot, spot, v.down_send_sem.at[part, step], v.down_recv_sem.at[part, step], down)

    def steps(part):
        return (4, 3) if part % 2 == 0 else (3, 4)

    def gather(part, step):
        for way, copy in enumerate((upward, downward)):
            if step and step - 1 < steps(part)[way]:
                copy(part, step - 1).wait_recv()
            if step < steps(part)[way]:
                copy(part, step).start()

    def pack(target, at):
        for s in range(8):
            parent = v.owners[at, along, s]
            source = parent // 8
            target(s, lax.rem(source // 2, Z), lax.rem(parent, 8))

    def across_copy(part, i):
        return send(
            v.packed.at[part, i],
            arrived[part].at[across],
            v.plane_send_sem.at[part, i],
            v.plane_recv_sem.at[part, i],
            plane[i][1],
        )

    def send_across(part):
        for i, (spot, _) in enumerate(plane):

            def put(s, z, j):
                v.packed[part, i, s] = lines[part][z, j]

            pack(put, spot)
            across_copy(part, i).start()

        def put(s, z, j):
            arrived[part][across, s] = lines[part][z, j]

        pack(put, across)

    listing.wait()
    for part in range(PARTS):
        own_two[part].wait()
        for copy in parts[part]:
            copy.wait_recv()
        gather(part, 0)
    for step in range(1, 6):
        if step < 5:
            gather(0, step)
        if step > 1:
            gather(1, step - 1)
        if step > 3:
            send_across(step - 4)
    for part in range(PARTS):
        for i in range(W - 1):
            across_copy(part, i).wait_recv()
        for s in range(8):
            source = v.owners[across, along, s] // 8
            two_out[s, part * half : (part + 1) * half, :] = arrived[part][2 * (source // 16) + lax.rem(source, 2), s]

    own_one.wait()
    for copy in ones:
        copy.wait()
    sent()
    for copy in halos + table_line + table_plane:
        copy.wait_send()
    for part in range(PARTS):
        for copy in parts[part]:
            copy.wait_send()
        for step in range(4):
            for way, copy in enumerate((upward, downward)):
                if step < steps(part)[way]:
                    copy(part, step).wait_send()
        for i in range(W - 1):
            across_copy(part, i).wait_send()


def local(panels, self_blocks, neighbors, skeleton_one, count_one, skeleton_two, count_two, parent_at_slot):
    hbm = pl.BlockSpec(memory_space=pl.ANY)
    vmem = pl.BlockSpec(memory_space=pltpu.VMEM)
    smem = pl.BlockSpec(memory_space=pltpu.SMEM)
    return pl.pallas_call(
        kernel,
        out_shape=[
            jax.ShapeDtypeStruct((BOXES, ROWS, SLOTS), F32),
            jax.ShapeDtypeStruct((8, ROWS, SLOTS), F32),
        ],
        in_specs=[hbm, hbm, hbm, vmem, smem, vmem, smem, smem],
        out_specs=[hbm, vmem],
        scratch_shapes=[
            pltpu.SMEM((BOXES, NEAR), jnp.int32),
            pltpu.SMEM((W, Z, SLOTS), jnp.int32),
            *(pltpu.VMEM(shape, dtype) for _, shape, dtype in SCRATCH),
            *(pltpu.SemaphoreType.DMA(shape) for _, shape in COPIES),
        ],
        compiler_params=pltpu.CompilerParams(collective_id=0, has_side_effects=True, vmem_limit_bytes=56 * MIB),
        name="skeletonize",
    )(panels, self_blocks, neighbors, skeleton_one, count_one, skeleton_two, count_two, parent_at_slot)


def solution(mesh):
    placed = (
        P("box", None, None),
        P("box", None, None),
        P("box", None),
        P("box", None),
        P("box"),
        P("box", None),
        P("box"),
        P("box"),
    )
    return jax.shard_map(
        local,
        mesh=mesh,
        in_specs=placed,
        out_specs=(P("box", "blk", None), P("box", "blk", None)),
        check_vma=False,
    )
```

```python
import jax
import jax.numpy as jnp
from jax import lax
from jax.experimental import pallas as pl
from jax.experimental.pallas import tpu as pltpu
from jax.sharding import PartitionSpec as P

STEPS = 3
MESH = pl.DeviceIdType.MESH
F32 = jnp.float32
BF16 = jnp.bfloat16
NN = (((1,), (0,)), ((), ()))
NT = (((1,), (1,)), ((), ()))
TN = (((0,), (0,)), ((), ()))
MIB = 1 << 20

HOMES, MEMBERS = 64, 4
BOXES, MINE = 16, 4
PANELS, SLOTS, NEAR = 256, 128, 8
Z, W = 8, 8
ROWS = SLOTS // MEMBERS
ROUND, OTHER = 0, 1


def halves(x):
    high = x.astype(BF16)
    return high, (x - high.astype(F32)).astype(BF16)


def dot(a, b, dims):
    return lax.dot_general(a, b, dims, preferred_element_type=F32)


def dot3(a, b, dims):
    return dot(a[0], b[0], dims) + (dot(a[0], b[1], dims) + dot(a[1], b[0], dims))


def square(a, dims):
    cross = dot(a[0], a[1], dims)
    return dot(a[0], a[0], dims) + (cross + cross.T)


def within(index, count):
    return jnp.minimum(jnp.maximum(index, 0), count - 1)


def place():
    home, member = lax.axis_index("box"), lax.axis_index("blk")
    return home, member


def enter(peers):
    barrier = pltpu.get_barrier_semaphore()
    for peer in peers:
        pl.semaphore_signal(barrier, inc=1, device_id=peer, device_id_type=MESH)
    pl.semaphore_wait(barrier, len(peers))


def send(source, target, send_sem, recv_sem, peer):
    return pltpu.make_async_remote_copy(
        src_ref=source,
        dst_ref=target,
        send_sem=send_sem,
        recv_sem=recv_sem,
        device_id=peer,
        device_id_type=MESH,
    )


def home_at(across, along):
    return (across // 2) * 16 + along * 2 + lax.rem(across, 2)


def lines_of(home, member):
    across = 2 * (home // 16) + lax.rem(home, 2)
    along = lax.rem(home // 2, Z)
    line = [(home_at(across, lax.rem(along + d, Z)), member) for d in range(1, Z)]
    spots = [lax.rem(across + d, W) for d in range(1, W)]
    plane = [(spot, (home_at(spot, along), member)) for spot in spots]
    return line, plane, across, along


def refine(gram, right, chosen):
    steps = [1.0 / jnp.max(jnp.sum(jnp.abs(g), axis=1, keepdims=True), axis=0, keepdims=True) for g in gram]
    grams = [halves(g) for g in gram]
    fits = list(chosen)
    for _ in range(STEPS):
        updates = [r - dot3(g, halves(f), NN) for g, r, f in zip(grams, right, fits)]
        fits = [f + s * u for f, s, u in zip(fits, steps, updates)]
    return fits


def chosen_columns(row, count):
    position = lax.broadcasted_iota(jnp.int32, (2 * SLOTS, SLOTS), 0)
    slot = lax.broadcasted_iota(jnp.int32, (2 * SLOTS, SLOTS), 1)
    return jnp.where((position == row) & (slot < count), 1.0, 0.0).astype(F32)


def normal(square_matrix, columns):
    picks = columns.T
    picks16 = picks.astype(BF16)
    columns16 = columns.astype(BF16)
    high, low = halves(square_matrix)
    right = dot(picks16, high, NN) + dot(picks16, low, NN)
    high, low = halves(right)
    gram = dot(high, columns16, NN) + dot(low, columns16, NN)
    return gram, right, picks


def couple(col, row):
    total = None
    for axis in range(3):
        offset = col[axis] - row[axis]
        total = offset * offset + (1024.0 * 0.01 if total is None else total)
    return lax.rsqrt(total)


SCRATCH = [
    ("window", (3 * BOXES, 4, PANELS), F32),
    ("column", (2, 3, PANELS, SLOTS), F32),
    ("couples", (MINE + 2, 2 * PANELS, NEAR * PANELS), BF16),
    ("siblings", (MINE // 2, 2 * PANELS, PANELS), BF16),
    ("fit_high", (MINE, SLOTS, PANELS), BF16),
    ("fit_low", (MINE, SLOTS, PANELS), BF16),
    ("left_high", (MINE, SLOTS, NEAR * PANELS), BF16),
    ("left_low", (MINE, SLOTS, NEAR * PANELS), BF16),
    ("reach", (10 * MINE, SLOTS, PANELS), F32),
    ("via", (MINE, SLOTS, PANELS), F32),
    ("round", (SLOTS, PANELS), F32),
    ("blocks", (MINE, PANELS, PANELS), F32),
    ("block", (MINE, SLOTS, SLOTS), F32),
    ("pair", (MINE // 2, SLOTS, SLOTS), F32),
    ("cross_high", (MINE, SLOTS, NEAR * SLOTS), BF16),
    ("cross_low", (MINE, SLOTS, NEAR * SLOTS), BF16),
    ("one", (MINE, SLOTS, SLOTS), F32),
    ("merged", (MINE // 2, PANELS, PANELS), F32),
    ("two", (MINE // 2, SLOTS, SLOTS), F32),
    ("mine", (16, SLOTS), F32),
    ("line_tables", (Z, 16, SLOTS), F32),
    ("ours", (8, SLOTS), jnp.int32),
    ("plane_tables", (W, 8, SLOTS), jnp.int32),
    ("answers", (W, 16, SLOTS), F32),
    ("heard", (W, 16, SLOTS), F32),
    ("lines00", (Z, MEMBERS, ROWS // 2, SLOTS), F32),
    ("lines01", (Z, MEMBERS, ROWS // 2, SLOTS), F32),
    ("lines10", (Z, MEMBERS, ROWS // 2, SLOTS), F32),
    ("lines11", (Z, MEMBERS, ROWS // 2, SLOTS), F32),
    ("packed", (2, W, 8, ROWS // 2, SLOTS), F32),
]
COPIES = [
    ("own", (9,)),
    ("halo_send", (2,)), ("halo_recv", (2,)),
    ("send", (7, MINE)), ("recv", (6, MINE)), ("give", (5, MINE)), ("take", (5, MINE)),
    ("table_send", (2, 7)), ("table_recv", (2, 7)), ("answer_send", (7,)), ("answer_recv", (7,)),
    ("row_send", (3,)), ("row_recv", (3,)), ("block_send", (4, 3)), ("block_recv", (4, 3)),
    ("up_send", (4, 4)), ("up_recv", (4, 4)), ("down_send", (4, 4)), ("down_recv", (4, 4)),
    ("plane_send", (2, 7)), ("plane_recv", (2, 7)),
]


class Refs:
    def __init__(self, refs):
        names = ["near", "owners"] + [name for name, *_ in SCRATCH] + [name + "_sem" for name, _ in COPIES]
        for name, ref in zip(names, refs, strict=True):
            setattr(self, name, ref)


def kernel(
    panels, self_blocks, neighbors, skeleton_one, count_one, skeleton_two, count_two, parent_at_slot, one_out, arrived, *refs
):
    v = Refs(refs)
    home, member = place()
    first = member * MINE
    boxes = range(MINE)
    side_hi, core = member // 2, lax.rem(member, 2)
    side_lo = lax.rem(home, 2)
    sign = 1 - 2 * side_hi
    outer = side_lo == side_hi
    flipped = home + 1 - 2 * side_lo
    side = (flipped, member)
    cross = (flipped, 2 * (1 - side_hi) + core)
    above = (lax.rem(home + 2 * sign + HOMES, HOMES), member)
    below = (lax.rem(home - 2 * sign + HOMES, HOMES), member)
    after = (lax.rem(home + 1, HOMES), member)
    before = (lax.rem(home + HOMES - 1, HOMES), member)
    sibling = (home, 2 * side_hi + 1 - core)
    members = [(home, lax.rem(member + d, MEMBERS)) for d in range(1, MEMBERS)]
    line, plane, across, along = lines_of(home, member)

    stage_near = pltpu.make_async_copy(neighbors, v.near, v.own_sem.at[0])
    stage_blocks = pltpu.make_async_copy(self_blocks.at[pl.ds(first, MINE)], v.blocks, v.own_sem.at[1])
    stage_panels = pltpu.make_async_copy(panels, v.window.at[pl.ds(BOXES, BOXES)], v.own_sem.at[2])
    stage_near.start()
    stage_panels.start()
    stage_blocks.start()

    lane = lax.broadcasted_iota(jnp.int32, (1, SLOTS), 1)
    nothing = jnp.full((1, SLOTS), -1.0, F32)
    owner_row, count_row, plain_row = nothing, nothing, jnp.zeros((1, SLOTS), jnp.int32)
    for s in range(8):
        owner_row = jnp.where(lane == 8 * along + s, parent_at_slot[s].astype(F32), owner_row)
        plain_row = jnp.where(lane == s, parent_at_slot[s], plain_row)
        count_row = jnp.where(lane == 8 * along + s, count_two[s].astype(F32), count_row)
    v.mine[0:8, :] = skeleton_two[...].astype(F32)
    v.mine[8:9, :] = owner_row
    v.mine[9:10, :] = count_row
    v.mine[10:16, :] = jnp.zeros((6, SLOTS), F32)
    v.ours[...] = jnp.broadcast_to(plain_row, (8, SLOTS))

    enter([after, before, cross, above, below] + members + line + [peer for _, peer in plane])

    halos = [
        send(panels, v.window.at[pl.ds(0, BOXES)], v.halo_send_sem.at[0], v.halo_recv_sem.at[0], after),
        send(panels, v.window.at[pl.ds(2 * BOXES, BOXES)], v.halo_send_sem.at[1], v.halo_recv_sem.at[1], before),
    ]
    for copy in halos:
        copy.start()

    spots = [(v.mine, v.line_tables.at[along]), (v.ours, v.plane_tables.at[across])]
    stage_tables = [pltpu.make_async_copy(*spot, v.own_sem.at[3 + i]) for i, spot in enumerate(spots)]
    tables = [
        send(*spots[way], v.table_send_sem.at[way, i], v.table_recv_sem.at[way, i], peer)
        for way, peers in enumerate((line, [peer for _, peer in plane]))
        for i, peer in enumerate(peers)
    ]
    answers = [
        send(v.answers.at[at], v.heard.at[across], v.answer_send_sem.at[i], v.answer_recv_sem.at[i], peer)
        for i, (at, peer) in enumerate(plane)
    ]
    listing = pltpu.make_async_copy(v.plane_tables.at[:, 0], v.owners, v.own_sem.at[5])

    def answer():
        for copy in tables:
            copy.wait_recv()
        for copy in stage_tables:
            copy.wait()
        listing.start()
        owner_row = jnp.max(v.line_tables[:, 8, :], axis=0, keepdims=True)
        count_row = jnp.max(v.line_tables[:, 9, :], axis=0, keepdims=True)
        row = lax.broadcasted_iota(jnp.int32, (8 * W, SLOTS), 0)
        at = row >> 3
        parent = 8 * ((at >> 1) * 16 + along * 2 + (at & 1)) + (row & 7)
        found = jnp.where(owner_row == parent.astype(F32), 1.0, 0.0).astype(F32)
        skeletons = jnp.concatenate([v.line_tables[z, 0:8, :] for z in range(Z)], axis=0)
        skeletons = jnp.concatenate([skeletons, jnp.zeros_like(skeletons)], axis=0)
        chosen = dot(found.astype(BF16), skeletons.astype(BF16), NN)
        counts = jnp.broadcast_to(jnp.sum(found * count_row, axis=1, keepdims=True), chosen.shape)
        for at in range(W):
            v.answers[at, 0:8, :] = chosen[8 * at : 8 * at + 8, :]
            v.answers[at, 8:16, :] = counts[8 * at : 8 * at + 8, :]
        v.heard[across] = v.answers[across]
        begin(answers)

    def begin(copies):
        for copy in copies:
            copy.start()

    begin(tables + stage_tables)

    def slot(shift, k, to=1):
        return v.reach.at[MINE * (2 * (2 + to * sign * shift) + core) + k]

    def moved(source, target, stream, k, peer, recv):
        return send(source, target, v.send_sem.at[stream, k], v.recv_sem.at[recv, k], peer)

    def passed(shift, i, k):
        return send(slot(shift, k), slot(shift, k), v.give_sem.at[i, k], v.take_sem.at[i, k], sibling)

    def arrival(stream, k):
        return moved(slot(0, k), slot(0, k), stream, k, side, stream)

    def at_outer(body):
        pl.when(outer)(body)

    def at_inner(body):
        pl.when(jnp.logical_not(outer))(body)

    def outer_moves(k):
        return {
            "own": [
                moved(slot(0, k), slot(-2, k), 0, k, side, 0),
                moved(slot(0, k), v.via.at[k], 1, k, below, 1),
            ]
            + ([moved(slot(0, k), v.round, 5, k, cross, 5)] if k == ROUND else []),
            "side": [moved(slot(2, k), slot(-2, k), 2, k, above, 2)]
            + ([moved(slot(2, k), slot(1, k, -1), 4, k, cross, 4)] if k == OTHER else []),
            "next": [moved(v.via.at[k], slot(-1, k, -1), 3, k, cross, 3)]
            + ([moved(v.round, slot(1, k), 6, k, side, 2)] if k == ROUND else []),
        }

    def inner_moves(k):
        return {
            "own": [
                moved(slot(0, k), slot(2, k), 0, k, side, 0),
                moved(slot(0, k), slot(-1, k, -1), 1, k, cross, 1),
            ],
            "side": ([moved(slot(-2, k), slot(1, k, -1), 2, k, cross, 2)] if k != ROUND else [])
            + [moved(slot(-2, k), slot(2, k), 3, k, below, 3)],
            "next": [moved(slot(-1, k), slot(1, k), 4, k, side, 4)] if k != OTHER else [],
        }

    def send_own(k):
        at_outer(lambda: begin(outer_moves(k)["own"]))
        at_inner(lambda: begin(inner_moves(k)["own"]))
        passed(0, 4, k).start()

    def early(k):
        @at_outer
        def _():
            arrival(0, k).wait_recv()
            begin(outer_moves(k)["side"] + [passed(2, 0, k)])
            arrival(1, k).wait_recv()
            if k == ROUND:
                arrival(5, k).wait_recv()
            begin(outer_moves(k)["next"])

        @at_inner
        def _():
            arrival(0, k).wait_recv()
            begin(inner_moves(k)["side"] + [passed(-2, 0, k)])
            arrival(1, k).wait_recv()
            begin(inner_moves(k)["next"] + [passed(-1, 1, k)])

    def late(k):
        @at_outer
        def _():
            for stream, shift, i in ((2, -2, 1), (3, -1, 2), (4, 1, 3)):
                arrival(stream, k).wait_recv()
                passed(shift, i, k).start()

        @at_inner
        def _():
            for stream, shift, i in ((2, 1, 2), (3, 2, 3)):
                arrival(stream, k).wait_recv()
                passed(shift, i, k).start()

    def taken():
        for k in boxes:
            for i in range(5):
                passed(0, i, k).wait_recv()

    def sent():
        for k in boxes:

            @at_outer
            def _():
                for copies in outer_moves(k).values():
                    for copy in copies:
                        copy.wait_send()

            @at_inner
            def _():
                for copies in inner_moves(k).values():
                    for copy in copies:
                        copy.wait_send()

            for i in range(5):
                passed(0, i, k).wait_send()

    tile = 64

    def columns_of(box, turn):
        for axis in range(3):
            row = 32.0 * v.window[BOXES + box, axis : axis + 1, :]
            v.column[turn, axis] = jnp.broadcast_to(row, (SLOTS, PANELS)).T

    def couple_with(turn, box, target, first_lane):
        for part in range(PANELS // SLOTS):
            lanes = slice(part * SLOTS, (part + 1) * SLOTS)
            row = [32.0 * v.window[box, axis : axis + 1, lanes] for axis in range(3)]
            lanes = slice(first_lane + part * SLOTS, first_lane + (part + 1) * SLOTS)
            for start in range(0, PANELS, tile):
                col = [v.column[turn, axis, start : start + tile, :] for axis in range(3)]
                hi, lo = halves(couple(col, row))
                target[start : start + tile, lanes] = hi
                target[PANELS + start : PANELS + start + tile, lanes] = lo

    order = [(first + k, slot(0, k), k) for k in boxes]

    def proxies(i, indices):
        box, _, room = order[i]
        for index in indices:
            near = within(v.near[index, box] - (home - 1) * BOXES, 3 * BOXES)
            couple_with(i % 2, near, v.couples.at[room], index * PANELS)

    def products(room, half):
        lanes = slice(half * (NEAR * PANELS // 2), (half + 1) * (NEAR * PANELS // 2))
        return dot(v.couples[room, :, lanes], v.couples[room, :PANELS, lanes], NT)

    def fit_box(i):
        box, spot, room = order[i]
        more = i + 1 < len(order)
        if more:
            columns_of(order[i + 1][0], (i + 1) % 2)
        total = products(room, 0)
        if more:
            proxies(i + 1, (0, 1, 2))
        total = total + products(room, 1)
        if more:
            proxies(i + 1, (3, 4, 5))
        low = total[PANELS:]
        columns = chosen_columns(skeleton_one[pl.ds(box, 1), :], count_one[box])
        gram, right, pick = normal(total[:PANELS] + (low + low.T), columns)
        (fit,) = refine([gram], [right], [pick])
        if more:
            proxies(i + 1, (6, 7))
        weight = jnp.sum(fit * fit * v.window[BOXES + box, 3:4, :], axis=1, keepdims=True)
        spot[...] = fit * lax.rsqrt(jnp.maximum(weight, 1.0))
        if i < MINE:
            v.fit_high[i], v.fit_low[i] = halves(fit)

    def split_fit(own):
        return v.fit_high[own], v.fit_low[own]

    def left_box(own):
        for index in range(NEAR):
            lanes = slice(index * PANELS, (index + 1) * PANELS)
            product = dot3(split_fit(own), (v.couples[own, :PANELS, lanes], v.couples[own, PANELS:, lanes]), NN)
            v.left_high[own, :, lanes], v.left_low[own, :, lanes] = halves(product)
        part = dot3(split_fit(own), halves(v.blocks[own]), NN)
        v.block[own] = dot3(halves(part), split_fit(own), NT)

    def pair_of(j):
        a, e = 2 * j, 2 * j + 1
        columns_of(first + a, j)
        couple_with(j, BOXES + first + e, v.siblings.at[j], 0)
        part = dot3(split_fit(a), (v.siblings[j, :PANELS, :], v.siblings[j, PANELS:, :]), NN)
        v.pair[j] = dot3(halves(part), split_fit(e), NT)

    stage_near.wait()
    stage_panels.wait()
    for copy in halos:
        copy.wait_recv()
    columns_of(first, 0)
    proxies(0, range(NEAR))
    fit_box(0)
    send_own(0)
    fit_box(1)
    send_own(1)
    answer()
    fit_box(2)
    send_own(2)
    fit_box(3)
    send_own(3)
    early(0)
    stage_blocks.wait()
    left_box(0)
    early(1)
    left_box(1)
    late(0)
    early(2)
    left_box(2)
    late(1)
    early(3)
    left_box(3)
    late(2)
    pair_of(0)
    pair_of(1)
    late(3)
    taken()

    base = 16 * home + 8 * side_hi - 16

    def level_one(own):
        for index in range(NEAR):
            box = within(v.near[index, first + own] - base, 10 * MINE)
            lanes = slice(index * PANELS, (index + 1) * PANELS)
            left = (v.left_high[own, :, lanes], v.left_low[own, :, lanes])
            lanes = slice(index * SLOTS, (index + 1) * SLOTS)
            v.cross_high[own, :, lanes], v.cross_low[own, :, lanes] = halves(dot3(left, halves(v.reach[box]), NT))
        v.one[own] = v.block[own] - square((v.cross_high[own], v.cross_low[own]), NT)

    def level_two(j):
        between = v.pair[j]
        v.merged[j, :SLOTS, :SLOTS] = v.one[2 * j]
        v.merged[j, :SLOTS, SLOTS:] = between
        v.merged[j, SLOTS:, :SLOTS] = between.T
        v.merged[j, SLOTS:, SLOTS:] = v.one[2 * j + 1]
        body = halves(v.merged[j])
        which = 2 * member + j
        row, count = v.heard[0, pl.ds(which, 1), :], v.heard[0, pl.ds(8 + which, 1), :]
        for at in range(1, W):
            row = row + v.heard[at, pl.ds(which, 1), :]
            count = count + v.heard[at, pl.ds(8 + which, 1), :]
        columns = chosen_columns(row.astype(jnp.int32), count.astype(jnp.int32))
        gram, right, pick = normal(square(body, TN), columns)
        (fit,) = refine([gram], [right], [pick])
        fit = halves(fit)
        v.two[j] = dot3(halves(dot3(fit, body, NN)), fit, NT)

    mine_one = one_out.at[pl.ds(MINE * member, MINE)]

    def one_rows(target):
        return v.one.at[:, pl.ds(pl.multiple_of(target * ROWS, ROWS), ROWS), :]

    own_one = pltpu.make_async_copy(one_rows(member), mine_one, v.own_sem.at[6])
    ones = [
        send(one_rows(peer[1]), mine_one, v.row_send_sem.at[i], v.row_recv_sem.at[i], peer)
        for i, peer in enumerate(members)
    ]

    up, down = line[0], line[-1]
    half = ROWS // 2
    lines = ((v.lines00, v.lines01), (v.lines10, v.lines11))

    def two_rows(j, part, target):
        return v.two.at[j, pl.ds(pl.multiple_of(target * ROWS + part * half, half), half), :]

    def member_copies(j, part):
        spot = lines[j][part].at[along, member]
        return [
            send(
                two_rows(j, part, peer[1]),
                spot,
                v.block_send_sem.at[2 * j + part, i],
                v.block_recv_sem.at[2 * j + part, i],
                peer,
            )
            for i, peer in enumerate(members)
        ]

    def upward(j, part, step):
        spot = lines[j][part].at[lax.rem(along - step + Z, Z)]
        return send(spot, spot, v.up_send_sem.at[2 * j + part, step], v.up_recv_sem.at[2 * j + part, step], up)

    def downward(j, part, step):
        spot = lines[j][part].at[lax.rem(along + step, Z)]
        return send(spot, spot, v.down_send_sem.at[2 * j + part, step], v.down_recv_sem.at[2 * j + part, step], down)

    def ways(part):
        return ((upward, 4), (downward, 3)) if part == 0 else ((upward, 3), (downward, 4))

    def share(j):
        for part in range(2):
            lines[j][part][along, member] = v.two[
                j, pl.ds(pl.multiple_of(member * ROWS + part * half, half), half), :
            ]
            begin(member_copies(j, part))

    def gather(j, part, step):
        if step == 0:
            for copy in member_copies(j, part):
                copy.wait_recv()
        for copy, count in ways(part):
            if 0 < step <= count:
                copy(j, part, step - 1).wait_recv()
            if step < count:
                copy(j, part, step).start()

    def pack(part, at):
        for s in range(8):
            parent = v.owners[at, s]
            z, m = lax.rem(parent // 16, Z), lax.rem(parent // 2, MEMBERS)
            odd = lax.rem(parent, 2)
            v.packed[part, at, s] = jnp.where(odd == 1, lines[1][part][z, m], lines[0][part][z, m])

    def across_copy(part, i):
        at, peer = plane[i]
        return send(
            v.packed.at[part, at],
            arrived.at[part, across],
            v.plane_send_sem.at[part, i],
            v.plane_recv_sem.at[part, i],
            peer,
        )

    own_across = [
        pltpu.make_async_copy(v.packed.at[part, across], arrived.at[part, across], v.own_sem.at[7 + part])
        for part in range(2)
    ]

    def send_across(part):
        for i, (at, _) in enumerate(plane):
            pack(part, at)
            across_copy(part, i).start()
        pack(part, across)
        own_across[part].start()

    for copy in answers:
        copy.wait_recv()
    level_one(0)
    level_one(1)
    level_two(0)
    share(0)
    level_one(2)
    level_one(3)
    level_two(1)
    share(1)
    begin(ones + [own_one])
    listing.wait()
    gather(0, 0, 0)
    gather(1, 0, 0)
    gather(0, 0, 1)
    gather(1, 0, 1)
    gather(0, 1, 0)
    gather(1, 1, 0)
    gather(0, 0, 2)
    gather(1, 0, 2)
    gather(0, 1, 1)
    gather(1, 1, 1)
    gather(0, 0, 3)
    gather(1, 0, 3)
    gather(0, 1, 2)
    gather(1, 1, 2)
    gather(0, 0, 4)
    gather(1, 0, 4)
    send_across(0)
    gather(0, 1, 3)
    gather(1, 1, 3)
    gather(0, 1, 4)
    gather(1, 1, 4)
    send_across(1)

    for part in range(2):
        for i in range(W - 1):
            across_copy(part, i).wait()
    for copy in own_across + [own_one] + ones:
        copy.wait()
    sent()
    for copy in halos + tables + answers:
        copy.wait_send()
    for j in range(2):
        for part in range(2):
            for copy in member_copies(j, part):
                copy.wait_send()
            for copy, count in ways(part):
                for step in range(count):
                    copy(j, part, step).wait_send()


def place_kernel(owners, one, arrived, one_out, two_out, sems):
    copies = [pltpu.make_async_copy(one, one_out, sems.at[16])]
    for s in range(8):
        source = owners[s] // 8
        at = 2 * (source // 16) + lax.rem(source, 2)
        for part in range(2):
            half = ROWS // 2
            copies.append(
                pltpu.make_async_copy(
                    arrived.at[part, at, s], two_out.at[s, pl.ds(part * half, half), :], sems.at[2 * s + part]
                )
            )
    for copy in copies:
        copy.start()
    for copy in copies:
        copy.wait()


def local(panels, self_blocks, neighbors, skeleton_one, count_one, skeleton_two, count_two, parent_at_slot):
    hbm = pl.BlockSpec(memory_space=pl.ANY)
    vmem = pl.BlockSpec(memory_space=pltpu.VMEM)
    smem = pl.BlockSpec(memory_space=pltpu.SMEM)
    one, arrived = pl.pallas_call(
        kernel,
        out_shape=[
            jax.ShapeDtypeStruct((BOXES, ROWS, SLOTS), F32),
            jax.ShapeDtypeStruct((2, W, 8, ROWS // 2, SLOTS), F32),
        ],
        in_specs=[hbm, hbm, hbm, vmem, smem, vmem, smem, smem],
        out_specs=[hbm, hbm],
        scratch_shapes=[
            pltpu.SMEM((NEAR, BOXES), jnp.int32),
            pltpu.SMEM((W, SLOTS), jnp.int32),
            *(pltpu.VMEM(shape, dtype) for _, shape, dtype in SCRATCH),
            *(pltpu.SemaphoreType.DMA(shape) for _, shape in COPIES),
        ],
        compiler_params=pltpu.CompilerParams(collective_id=0, has_side_effects=True, vmem_limit_bytes=56 * MIB),
        name="skeletonize",
    )(panels, self_blocks, neighbors.T, skeleton_one, count_one, skeleton_two, count_two, parent_at_slot)
    return pl.pallas_call(
        place_kernel,
        out_shape=[
            jax.ShapeDtypeStruct((BOXES, ROWS, SLOTS), F32),
            jax.ShapeDtypeStruct((8, ROWS, SLOTS), F32),
        ],
        in_specs=[smem, hbm, hbm],
        out_specs=[vmem, vmem],
        scratch_shapes=[pltpu.SemaphoreType.DMA((17,))],
        compiler_params=pltpu.CompilerParams(vmem_limit_bytes=56 * MIB),
        name="place",
    )(parent_at_slot, one, arrived)


def solution(mesh):
    placed = (
        P("box", None, None),
        P("box", None, None),
        P("box", None),
        P("box", None),
        P("box"),
        P("box", None),
        P("box"),
        P("box"),
    )
    return jax.shard_map(
        local,
        mesh=mesh,
        in_specs=placed,
        out_specs=(P("box", "blk", None), P("box", "blk", None)),
        check_vma=False,
    )
```

```python
import jax
import jax.numpy as jnp
from jax import lax
from jax.experimental import pallas as pl
from jax.experimental.pallas import tpu as pltpu
from jax.sharding import PartitionSpec as P

STEPS = 3
MESH = pl.DeviceIdType.MESH
F32 = jnp.float32
BF16 = jnp.bfloat16
NN = (((1,), (0,)), ((), ()))
NT = (((1,), (1,)), ((), ()))
TN = (((0,), (0,)), ((), ()))
MIB = 1 << 20

HOMES, MEMBERS = 64, 4
BOXES, MINE = 16, 4
PANELS, SLOTS, NEAR = 256, 128, 8
Z, W = 8, 8
ROWS = SLOTS // MEMBERS
ROUND, OTHER = 0, 1


def halves(x):
    high = x.astype(BF16)
    return high, (x - high.astype(F32)).astype(BF16)


def dot(a, b, dims):
    return lax.dot_general(a, b, dims, preferred_element_type=F32)


def dot3(a, b, dims):
    return dot(a[0], b[0], dims) + (dot(a[0], b[1], dims) + dot(a[1], b[0], dims))


def square(a, dims):
    cross = dot(a[0], a[1], dims)
    return dot(a[0], a[0], dims) + (cross + cross.T)


def within(index, count):
    return jnp.minimum(jnp.maximum(index, 0), count - 1)


def place():
    home, member = lax.axis_index("box"), lax.axis_index("blk")
    return home, member


def send(source, target, send_sem, recv_sem, peer):
    return pltpu.make_async_remote_copy(
        src_ref=source,
        dst_ref=target,
        send_sem=send_sem,
        recv_sem=recv_sem,
        device_id=peer,
        device_id_type=MESH,
    )


def home_at(across, along):
    return (across // 2) * 16 + along * 2 + lax.rem(across, 2)


def lines_of(home, member):
    across = 2 * (home // 16) + lax.rem(home, 2)
    along = lax.rem(home // 2, Z)
    line = [(home_at(across, lax.rem(along + d, Z)), member) for d in range(1, Z)]
    spots = [lax.rem(across + d, W) for d in range(1, W)]
    plane = [(spot, (home_at(spot, along), member)) for spot in spots]
    return line, plane, across, along


def refine(gram, right, chosen):
    steps = [1.0 / jnp.max(jnp.sum(jnp.abs(g), axis=1, keepdims=True), axis=0, keepdims=True) for g in gram]
    grams = [halves(g) for g in gram]
    fits = list(chosen)
    for _ in range(STEPS):
        updates = [r - dot3(g, halves(f), NN) for g, r, f in zip(grams, right, fits)]
        fits = [f + s * u for f, s, u in zip(fits, steps, updates)]
    return fits


def chosen_columns(row, count):
    position = lax.broadcasted_iota(jnp.int32, (2 * SLOTS, SLOTS), 0)
    slot = lax.broadcasted_iota(jnp.int32, (2 * SLOTS, SLOTS), 1)
    return jnp.where((position == row) & (slot < count), 1.0, 0.0).astype(F32)


def normal(square_matrix, columns):
    picks = columns.T
    picks16 = picks.astype(BF16)
    columns16 = columns.astype(BF16)
    high, low = halves(square_matrix)
    right = dot(picks16, high, NN) + dot(picks16, low, NN)
    high, low = halves(right)
    gram = dot(high, columns16, NN) + dot(low, columns16, NN)
    return gram, right, picks


def couple(col, row):
    total = None
    for axis in range(3):
        offset = col[axis] - row[axis]
        total = offset * offset + (1024.0 * 0.01 if total is None else total)
    return lax.rsqrt(total)


SCRATCH = [
    ("skeleton_one", (BOXES, SLOTS), jnp.int32),
    ("skeleton_two", (8, SLOTS), jnp.int32),
    ("window", (3 * BOXES, 4, PANELS), F32),
    ("column", (2, 3, PANELS, SLOTS), F32),
    ("couples", (MINE + 2, 2 * PANELS, NEAR * PANELS), BF16),
    ("siblings", (MINE // 2, 2 * PANELS, PANELS), BF16),
    ("fit_high", (MINE, SLOTS, PANELS), BF16),
    ("fit_low", (MINE, SLOTS, PANELS), BF16),
    ("left_high", (MINE, SLOTS, NEAR * PANELS), BF16),
    ("left_low", (MINE, SLOTS, NEAR * PANELS), BF16),
    ("reach", (10 * MINE, SLOTS, PANELS), F32),
    ("via", (MINE, SLOTS, PANELS), F32),
    ("round", (SLOTS, PANELS), F32),
    ("blocks", (MINE, PANELS, PANELS), F32),
    ("block", (MINE, SLOTS, SLOTS), F32),
    ("pair", (MINE // 2, SLOTS, SLOTS), F32),
    ("cross_high", (MINE, SLOTS, NEAR * SLOTS), BF16),
    ("cross_low", (MINE, SLOTS, NEAR * SLOTS), BF16),
    ("one", (MINE, SLOTS, SLOTS), F32),
    ("merged", (MINE // 2, PANELS, PANELS), F32),
    ("two", (MINE // 2, SLOTS, SLOTS), F32),
    ("mine", (16, SLOTS), F32),
    ("line_tables", (Z, 16, SLOTS), F32),
    ("ours", (8, SLOTS), jnp.int32),
    ("plane_tables", (W, 8, SLOTS), jnp.int32),
    ("answers", (W, 16, SLOTS), F32),
    ("heard", (W, 16, SLOTS), F32),
    ("lines00", (Z, MEMBERS, ROWS // 2, SLOTS), F32),
    ("lines01", (Z, MEMBERS, ROWS // 2, SLOTS), F32),
    ("lines10", (Z, MEMBERS, ROWS // 2, SLOTS), F32),
    ("lines11", (Z, MEMBERS, ROWS // 2, SLOTS), F32),
    ("packed", (2, W, 8, ROWS // 2, SLOTS), F32),
]
COPIES = [
    ("own", (9,)), ("stage", (2,)),
    ("halo_send", (2, 4)), ("halo_recv", (2, 4)),
    ("send", (7, MINE)), ("recv", (6, MINE)), ("give", (5, MINE)), ("take", (5, MINE)),
    ("table_send", (2, 7)), ("table_recv", (2, 7)), ("answer_send", (7,)), ("answer_recv", (7,)),
    ("row_send", (3,)), ("row_recv", (3,)), ("block_send", (4, 3)), ("block_recv", (4, 3)),
    ("up_send", (4, 4)), ("up_recv", (4, 4)), ("down_send", (4, 4)), ("down_recv", (4, 4)),
    ("plane_send", (2, 7)), ("plane_recv", (2, 7)),
]


class Refs:
    def __init__(self, refs):
        names = ["near", "owners"] + [name for name, *_ in SCRATCH] + [name + "_sem" for name, _ in COPIES]
        for name, ref in zip(names, refs, strict=True):
            setattr(self, name, ref)


def kernel(
    panels, self_blocks, neighbors, skeleton_one, count_one, skeleton_two, count_two, parent_at_slot, one_out, arrived, *refs
):
    v = Refs(refs)
    home, member = place()
    first = member * MINE
    boxes = range(MINE)
    side_hi, core = member // 2, lax.rem(member, 2)
    side_lo = lax.rem(home, 2)
    sign = 1 - 2 * side_hi
    outer = side_lo == side_hi
    flipped = home + 1 - 2 * side_lo
    side = (flipped, member)
    cross = (flipped, 2 * (1 - side_hi) + core)
    above = (lax.rem(home + 2 * sign + HOMES, HOMES), member)
    below = (lax.rem(home - 2 * sign + HOMES, HOMES), member)
    after = (lax.rem(home + 1, HOMES), member)
    before = (lax.rem(home + HOMES - 1, HOMES), member)
    sibling = (home, 2 * side_hi + 1 - core)
    members = [(home, lax.rem(member + d, MEMBERS)) for d in range(1, MEMBERS)]
    line, plane, across, along = lines_of(home, member)

    barrier = pltpu.get_barrier_semaphore()
    peers = [after, before, cross, above, below] + members + line + [peer for _, peer in plane]
    for peer in peers:
        pl.semaphore_signal(barrier, inc=1, device_id=peer, device_id_type=MESH)

    stage_near = pltpu.make_async_copy(neighbors, v.near, v.own_sem.at[0])
    stage_blocks = pltpu.make_async_copy(self_blocks.at[pl.ds(first, MINE)], v.blocks, v.own_sem.at[1])
    stage_panels = pltpu.make_async_copy(panels, v.window.at[pl.ds(BOXES, BOXES)], v.own_sem.at[2])
    stage_two = pltpu.make_async_copy(skeleton_two, v.skeleton_two, v.stage_sem.at[0])
    stage_one = pltpu.make_async_copy(skeleton_one, v.skeleton_one, v.stage_sem.at[1])
    for copy in (stage_near, stage_panels, stage_two, stage_one, stage_blocks):
        copy.start()

    pl.semaphore_wait(barrier, len(peers))

    def halo(way, piece):
        boxes_of = pl.ds(MINE * piece, MINE)
        room = pl.ds(2 * BOXES * way + MINE * piece, MINE)
        return send(
            panels.at[boxes_of],
            v.window.at[room],
            v.halo_send_sem.at[way, piece],
            v.halo_recv_sem.at[way, piece],
            (after, before)[way],
        )

    def halos(act):
        for piece in range(MEMBERS):
            pl.when(piece >= member)(lambda: act(halo(0, piece)))
            pl.when(piece <= member)(lambda: act(halo(1, piece)))

    halos(lambda copy: copy.start())

    lane = lax.broadcasted_iota(jnp.int32, (1, SLOTS), 1)
    nothing = jnp.full((1, SLOTS), -1.0, F32)
    owner_row, count_row, plain_row = nothing, nothing, jnp.zeros((1, SLOTS), jnp.int32)
    for s in range(8):
        owner_row = jnp.where(lane == 8 * along + s, parent_at_slot[s].astype(F32), owner_row)
        plain_row = jnp.where(lane == s, parent_at_slot[s], plain_row)
        count_row = jnp.where(lane == 8 * along + s, count_two[s].astype(F32), count_row)
    stage_two.wait()
    v.mine[0:8, :] = v.skeleton_two[...].astype(F32)
    v.mine[8:9, :] = owner_row
    v.mine[9:10, :] = count_row
    v.mine[10:16, :] = jnp.zeros((6, SLOTS), F32)
    v.ours[...] = jnp.broadcast_to(plain_row, (8, SLOTS))

    spots = [(v.mine, v.line_tables.at[along]), (v.ours, v.plane_tables.at[across])]
    stage_tables = [pltpu.make_async_copy(*spot, v.own_sem.at[3 + i]) for i, spot in enumerate(spots)]
    tables = [
        send(*spots[way], v.table_send_sem.at[way, i], v.table_recv_sem.at[way, i], peer)
        for way, peers in enumerate((line, [peer for _, peer in plane]))
        for i, peer in enumerate(peers)
    ]
    answers = [
        send(v.answers.at[at], v.heard.at[across], v.answer_send_sem.at[i], v.answer_recv_sem.at[i], peer)
        for i, (at, peer) in enumerate(plane)
    ]
    listing = pltpu.make_async_copy(v.plane_tables.at[:, 0], v.owners, v.own_sem.at[5])

    def answer():
        for copy in tables:
            copy.wait_recv()
        for copy in stage_tables:
            copy.wait()
        listing.start()
        owner_row = jnp.max(v.line_tables[:, 8, :], axis=0, keepdims=True)
        count_row = jnp.max(v.line_tables[:, 9, :], axis=0, keepdims=True)
        row = lax.broadcasted_iota(jnp.int32, (8 * W, SLOTS), 0)
        at = row >> 3
        parent = 8 * ((at >> 1) * 16 + along * 2 + (at & 1)) + (row & 7)
        found = jnp.where(owner_row == parent.astype(F32), 1.0, 0.0).astype(F32)
        skeletons = jnp.concatenate([v.line_tables[z, 0:8, :] for z in range(Z)], axis=0)
        skeletons = jnp.concatenate([skeletons, jnp.zeros_like(skeletons)], axis=0)
        chosen = dot(found.astype(BF16), skeletons.astype(BF16), NN)
        counts = jnp.broadcast_to(jnp.sum(found * count_row, axis=1, keepdims=True), chosen.shape)
        for at in range(W):
            v.answers[at, 0:8, :] = chosen[8 * at : 8 * at + 8, :]
            v.answers[at, 8:16, :] = counts[8 * at : 8 * at + 8, :]
        v.heard[across] = v.answers[across]
        begin(answers)

    def begin(copies):
        for copy in copies:
            copy.start()

    begin(tables + stage_tables)

    def slot(shift, k, to=1):
        return v.reach.at[MINE * (2 * (2 + to * sign * shift) + core) + k]

    def moved(source, target, stream, k, peer, recv):
        return send(source, target, v.send_sem.at[stream, k], v.recv_sem.at[recv, k], peer)

    def passed(shift, i, k):
        return send(slot(shift, k), slot(shift, k), v.give_sem.at[i, k], v.take_sem.at[i, k], sibling)

    def arrival(stream, k):
        return moved(slot(0, k), slot(0, k), stream, k, side, stream)

    def at_outer(body):
        pl.when(outer)(body)

    def at_inner(body):
        pl.when(jnp.logical_not(outer))(body)

    def outer_moves(k):
        return {
            "own": [
                moved(slot(0, k), slot(-2, k), 0, k, side, 0),
                moved(slot(0, k), v.via.at[k], 1, k, below, 1),
            ]
            + ([moved(slot(0, k), v.round, 5, k, cross, 5)] if k == ROUND else []),
            "side": [moved(slot(2, k), slot(-2, k), 2, k, above, 2)]
            + ([moved(slot(2, k), slot(1, k, -1), 4, k, cross, 4)] if k == OTHER else []),
            "next": [moved(v.via.at[k], slot(-1, k, -1), 3, k, cross, 3)]
            + ([moved(v.round, slot(1, k), 6, k, side, 2)] if k == ROUND else []),
        }

    def inner_moves(k):
        return {
            "own": [
                moved(slot(0, k), slot(2, k), 0, k, side, 0),
                moved(slot(0, k), slot(-1, k, -1), 1, k, cross, 1),
            ],
            "side": ([moved(slot(-2, k), slot(1, k, -1), 2, k, cross, 2)] if k != ROUND else [])
            + [moved(slot(-2, k), slot(2, k), 3, k, below, 3)],
            "next": [moved(slot(-1, k), slot(1, k), 4, k, side, 4)] if k != OTHER else [],
        }

    def send_own(k):
        at_outer(lambda: begin(outer_moves(k)["own"]))
        at_inner(lambda: begin(inner_moves(k)["own"]))
        passed(0, 4, k).start()

    def early(k):
        @at_outer
        def _():
            arrival(0, k).wait_recv()
            begin(outer_moves(k)["side"] + [passed(2, 0, k)])
            arrival(1, k).wait_recv()
            if k == ROUND:
                arrival(5, k).wait_recv()
            begin(outer_moves(k)["next"])

        @at_inner
        def _():
            arrival(0, k).wait_recv()
            begin(inner_moves(k)["side"] + [passed(-2, 0, k)])
            arrival(1, k).wait_recv()
            begin(inner_moves(k)["next"] + [passed(-1, 1, k)])

    def late(k):
        @at_outer
        def _():
            for stream, shift, i in ((2, -2, 1), (3, -1, 2), (4, 1, 3)):
                arrival(stream, k).wait_recv()
                passed(shift, i, k).start()

        @at_inner
        def _():
            for stream, shift, i in ((2, 1, 2), (3, 2, 3)):
                arrival(stream, k).wait_recv()
                passed(shift, i, k).start()

    def taken():
        for k in boxes:
            for i in range(5):
                passed(0, i, k).wait_recv()

    def sent():
        for k in boxes:

            @at_outer
            def _():
                for copies in outer_moves(k).values():
                    for copy in copies:
                        copy.wait_send()

            @at_inner
            def _():
                for copies in inner_moves(k).values():
                    for copy in copies:
                        copy.wait_send()

            for i in range(5):
                passed(0, i, k).wait_send()

    tile = 64

    def columns_of(box, turn):
        for axis in range(3):
            row = 32.0 * v.window[BOXES + box, axis : axis + 1, :]
            v.column[turn, axis] = jnp.broadcast_to(row, (SLOTS, PANELS)).T

    def couple_with(turn, box, target, first_lane):
        for part in range(PANELS // SLOTS):
            lanes = slice(part * SLOTS, (part + 1) * SLOTS)
            row = [32.0 * v.window[box, axis : axis + 1, lanes] for axis in range(3)]
            lanes = slice(first_lane + part * SLOTS, first_lane + (part + 1) * SLOTS)
            for start in range(0, PANELS, tile):
                col = [v.column[turn, axis, start : start + tile, :] for axis in range(3)]
                hi, lo = halves(couple(col, row))
                target[start : start + tile, lanes] = hi
                target[PANELS + start : PANELS + start + tile, lanes] = lo

    order = [(first + k, slot(0, k), k) for k in boxes]

    def proxies(i, indices):
        box, _, room = order[i]
        for index in indices:
            near = within(v.near[index, box] - (home - 1) * BOXES, 3 * BOXES)
            couple_with(i % 2, near, v.couples.at[room], index * PANELS)

    def products(room, half):
        lanes = slice(half * (NEAR * PANELS // 2), (half + 1) * (NEAR * PANELS // 2))
        return dot(v.couples[room, :, lanes], v.couples[room, :PANELS, lanes], NT)

    def fit_box(i):
        box, spot, room = order[i]
        more = 0 < i < len(order) - 1
        if more:
            columns_of(order[i + 1][0], (i + 1) % 2)
        total = products(room, 0)
        if more:
            proxies(i + 1, (0, 1, 2))
        total = total + products(room, 1)
        if more:
            proxies(i + 1, (3, 4, 5))
        low = total[PANELS:]
        columns = chosen_columns(v.skeleton_one[pl.ds(box, 1), :], count_one[box])
        gram, right, pick = normal(total[:PANELS] + (low + low.T), columns)
        (fit,) = refine([gram], [right], [pick])
        if more:
            proxies(i + 1, (6, 7))
        weight = jnp.sum(fit * fit * v.window[BOXES + box, 3:4, :], axis=1, keepdims=True)
        spot[...] = fit * lax.rsqrt(jnp.maximum(weight, 1.0))
        if i < MINE:
            v.fit_high[i], v.fit_low[i] = halves(fit)

    def split_fit(own):
        return v.fit_high[own], v.fit_low[own]

    def left_box(own):
        for index in range(NEAR):
            lanes = slice(index * PANELS, (index + 1) * PANELS)
            product = dot3(split_fit(own), (v.couples[own, :PANELS, lanes], v.couples[own, PANELS:, lanes]), NN)
            v.left_high[own, :, lanes], v.left_low[own, :, lanes] = halves(product)
        part = dot3(split_fit(own), halves(v.blocks[own]), NN)
        v.block[own] = dot3(halves(part), split_fit(own), NT)

    def pair_of(j):
        a, e = 2 * j, 2 * j + 1
        columns_of(first + a, j)
        couple_with(j, BOXES + first + e, v.siblings.at[j], 0)
        part = dot3(split_fit(a), (v.siblings[j, :PANELS, :], v.siblings[j, PANELS:, :]), NN)
        v.pair[j] = dot3(halves(part), split_fit(e), NT)

    stage_near.wait()
    stage_one.wait()
    stage_panels.wait()
    halos(lambda copy: copy.wait_recv())
    columns_of(first, 0)
    proxies(0, range(NEAR))
    fit_box(0)
    send_own(0)
    columns_of(first + 1, 1)
    proxies(1, range(NEAR))
    fit_box(1)
    send_own(1)
    early(0)
    answer()
    fit_box(2)
    send_own(2)
    early(1)
    late(0)
    fit_box(3)
    send_own(3)
    early(2)
    late(1)
    stage_blocks.wait()
    left_box(0)
    left_box(1)
    early(3)
    late(2)
    pair_of(0)
    left_box(2)
    left_box(3)
    pair_of(1)
    late(3)
    taken()

    base = 16 * home + 8 * side_hi - 16

    def level_one(own):
        for index in range(NEAR):
            box = within(v.near[index, first + own] - base, 10 * MINE)
            lanes = slice(index * PANELS, (index + 1) * PANELS)
            left = (v.left_high[own, :, lanes], v.left_low[own, :, lanes])
            lanes = slice(index * SLOTS, (index + 1) * SLOTS)
            v.cross_high[own, :, lanes], v.cross_low[own, :, lanes] = halves(dot3(left, halves(v.reach[box]), NT))
        v.one[own] = v.block[own] - square((v.cross_high[own], v.cross_low[own]), NT)

    def level_two(j):
        between = v.pair[j]
        v.merged[j, :SLOTS, :SLOTS] = v.one[2 * j]
        v.merged[j, :SLOTS, SLOTS:] = between
        v.merged[j, SLOTS:, :SLOTS] = between.T
        v.merged[j, SLOTS:, SLOTS:] = v.one[2 * j + 1]
        body = halves(v.merged[j])
        which = 2 * member + j
        row, count = v.heard[0, pl.ds(which, 1), :], v.heard[0, pl.ds(8 + which, 1), :]
        for at in range(1, W):
            row = row + v.heard[at, pl.ds(which, 1), :]
            count = count + v.heard[at, pl.ds(8 + which, 1), :]
        columns = chosen_columns(row.astype(jnp.int32), count.astype(jnp.int32))
        gram, right, pick = normal(square(body, TN), columns)
        (fit,) = refine([gram], [right], [pick])
        fit = halves(fit)
        v.two[j] = dot3(halves(dot3(fit, body, NN)), fit, NT)

    mine_one = one_out.at[pl.ds(MINE * member, MINE)]

    def one_rows(target):
        return v.one.at[:, pl.ds(pl.multiple_of(target * ROWS, ROWS), ROWS), :]

    own_one = pltpu.make_async_copy(one_rows(member), mine_one, v.own_sem.at[6])
    ones = [
        send(one_rows(peer[1]), mine_one, v.row_send_sem.at[i], v.row_recv_sem.at[i], peer)
        for i, peer in enumerate(members)
    ]

    up, down = line[0], line[-1]
    half = ROWS // 2
    lines = ((v.lines00, v.lines01), (v.lines10, v.lines11))

    def two_rows(j, part, target):
        return v.two.at[j, pl.ds(pl.multiple_of(target * ROWS + part * half, half), half), :]

    def member_copies(j, part):
        spot = lines[j][part].at[along, member]
        return [
            send(
                two_rows(j, part, peer[1]),
                spot,
                v.block_send_sem.at[2 * j + part, i],
                v.block_recv_sem.at[2 * j + part, i],
                peer,
            )
            for i, peer in enumerate(members)
        ]

    def upward(j, part, step):
        spot = lines[j][part].at[lax.rem(along - step + Z, Z)]
        return send(spot, spot, v.up_send_sem.at[2 * j + part, step], v.up_recv_sem.at[2 * j + part, step], up)

    def downward(j, part, step):
        spot = lines[j][part].at[lax.rem(along + step, Z)]
        return send(spot, spot, v.down_send_sem.at[2 * j + part, step], v.down_recv_sem.at[2 * j + part, step], down)

    def ways(part):
        return ((upward, 4), (downward, 3)) if part == 0 else ((upward, 3), (downward, 4))

    def share(j):
        for part in range(2):
            lines[j][part][along, member] = v.two[
                j, pl.ds(pl.multiple_of(member * ROWS + part * half, half), half), :
            ]
            begin(member_copies(j, part))

    def gather(j, part, step):
        if step == 0:
            for copy in member_copies(j, part):
                copy.wait_recv()
        for copy, count in ways(part):
            if 0 < step <= count:
                copy(j, part, step - 1).wait_recv()
            if step < count:
                copy(j, part, step).start()

    def pack(part, at):
        for s in range(8):
            parent = v.owners[at, s]
            z, m = lax.rem(parent // 16, Z), lax.rem(parent // 2, MEMBERS)
            odd = lax.rem(parent, 2)
            v.packed[part, at, s] = jnp.where(odd == 1, lines[1][part][z, m], lines[0][part][z, m])

    def across_copy(part, i):
        at, peer = plane[i]
        return send(
            v.packed.at[part, at],
            arrived.at[part, across],
            v.plane_send_sem.at[part, i],
            v.plane_recv_sem.at[part, i],
            peer,
        )

    own_across = [
        pltpu.make_async_copy(v.packed.at[part, across], arrived.at[part, across], v.own_sem.at[7 + part])
        for part in range(2)
    ]

    def send_across(part):
        for i, (at, _) in enumerate(plane):
            pack(part, at)
            across_copy(part, i).start()
        pack(part, across)
        own_across[part].start()

    for copy in answers:
        copy.wait_recv()
    level_one(0)
    level_one(1)
    level_two(0)
    share(0)
    level_one(2)
    level_one(3)
    level_two(1)
    share(1)
    begin(ones + [own_one])
    listing.wait()
    gather(0, 0, 0)
    gather(1, 0, 0)
    gather(0, 0, 1)
    gather(1, 0, 1)
    gather(0, 1, 0)
    gather(1, 1, 0)
    gather(0, 0, 2)
    gather(1, 0, 2)
    gather(0, 1, 1)
    gather(1, 1, 1)
    gather(0, 0, 3)
    gather(1, 0, 3)
    gather(0, 1, 2)
    gather(1, 1, 2)
    gather(0, 0, 4)
    gather(1, 0, 4)
    send_across(0)
    gather(0, 1, 3)
    gather(1, 1, 3)
    gather(0, 1, 4)
    gather(1, 1, 4)
    send_across(1)

    for part in range(2):
        for i in range(W - 1):
            across_copy(part, i).wait()
    for copy in own_across + [own_one] + ones:
        copy.wait()
    sent()
    halos(lambda copy: copy.wait_send())
    for copy in tables + answers:
        copy.wait_send()
    for j in range(2):
        for part in range(2):
            for copy in member_copies(j, part):
                copy.wait_send()
            for copy, count in ways(part):
                for step in range(count):
                    copy(j, part, step).wait_send()


def place_kernel(owners, one, arrived, one_out, two_out, sems):
    copies = [pltpu.make_async_copy(one, one_out, sems.at[16])]
    for s in range(8):
        source = owners[s] // 8
        at = 2 * (source // 16) + lax.rem(source, 2)
        for part in range(2):
            half = ROWS // 2
            copies.append(
                pltpu.make_async_copy(
                    arrived.at[part, at, s], two_out.at[s, pl.ds(part * half, half), :], sems.at[2 * s + part]
                )
            )
    for copy in copies:
        copy.start()
    for copy in copies:
        copy.wait()


def local(panels, self_blocks, neighbors, skeleton_one, count_one, skeleton_two, count_two, parent_at_slot):
    hbm = pl.BlockSpec(memory_space=pl.ANY)
    vmem = pl.BlockSpec(memory_space=pltpu.VMEM)
    smem = pl.BlockSpec(memory_space=pltpu.SMEM)
    one, arrived = pl.pallas_call(
        kernel,
        out_shape=[
            jax.ShapeDtypeStruct((BOXES, ROWS, SLOTS), F32),
            jax.ShapeDtypeStruct((2, W, 8, ROWS // 2, SLOTS), F32),
        ],
        in_specs=[hbm, hbm, hbm, hbm, smem, hbm, smem, smem],
        out_specs=[hbm, hbm],
        scratch_shapes=[
            pltpu.SMEM((NEAR, BOXES), jnp.int32),
            pltpu.SMEM((W, SLOTS), jnp.int32),
            *(pltpu.VMEM(shape, dtype) for _, shape, dtype in SCRATCH),
            *(pltpu.SemaphoreType.DMA(shape) for _, shape in COPIES),
        ],
        compiler_params=pltpu.CompilerParams(collective_id=0, has_side_effects=True, vmem_limit_bytes=56 * MIB),
        name="skeletonize",
    )(panels, self_blocks, neighbors.T, skeleton_one, count_one, skeleton_two, count_two, parent_at_slot)
    return pl.pallas_call(
        place_kernel,
        out_shape=[
            jax.ShapeDtypeStruct((BOXES, ROWS, SLOTS), F32),
            jax.ShapeDtypeStruct((8, ROWS, SLOTS), F32),
        ],
        in_specs=[smem, hbm, hbm],
        out_specs=[vmem, vmem],
        scratch_shapes=[pltpu.SemaphoreType.DMA((17,))],
        compiler_params=pltpu.CompilerParams(vmem_limit_bytes=56 * MIB),
        name="place",
    )(parent_at_slot, one, arrived)


def solution(mesh):
    placed = (
        P("box", None, None),
        P("box", None, None),
        P("box", None),
        P("box", None),
        P("box"),
        P("box", None),
        P("box"),
        P("box"),
    )
    return jax.shard_map(
        local,
        mesh=mesh,
        in_specs=placed,
        out_specs=(P("box", "blk", None), P("box", "blk", None)),
        check_vma=False,
    )
```

```python
import jax
import jax.numpy as jnp
from jax import lax
from jax.experimental import pallas as pl
from jax.experimental.pallas import tpu as pltpu
from jax.sharding import PartitionSpec as P

STEPS = 3
MESH = pl.DeviceIdType.MESH
F32 = jnp.float32
BF16 = jnp.bfloat16
NN = (((1,), (0,)), ((), ()))
NT = (((1,), (1,)), ((), ()))
TN = (((0,), (0,)), ((), ()))
MIB = 1 << 20

HOMES, MEMBERS = 64, 4
BOXES, MINE = 16, 4
PANELS, SLOTS, NEAR = 256, 128, 8
Z, W = 8, 8
ROWS = SLOTS // MEMBERS
ROUND, OTHER = 0, 1


def halves(x):
    high = x.astype(BF16)
    return high, (x - high.astype(F32)).astype(BF16)


def dot(a, b, dims):
    return lax.dot_general(a, b, dims, preferred_element_type=F32)


def dot3(a, b, dims):
    return dot(a[0], b[0], dims) + (dot(a[0], b[1], dims) + dot(a[1], b[0], dims))


def square(a, dims):
    cross = dot(a[0], a[1], dims)
    return dot(a[0], a[0], dims) + (cross + cross.T)


def within(index, count):
    return jnp.minimum(jnp.maximum(index, 0), count - 1)


def place():
    home, member = lax.axis_index("box"), lax.axis_index("blk")
    return home, member


def send(source, target, send_sem, recv_sem, peer):
    return pltpu.make_async_remote_copy(
        src_ref=source,
        dst_ref=target,
        send_sem=send_sem,
        recv_sem=recv_sem,
        device_id=peer,
        device_id_type=MESH,
    )


def home_at(across, along):
    return (across // 2) * 16 + along * 2 + lax.rem(across, 2)


def lines_of(home, member):
    across = 2 * (home // 16) + lax.rem(home, 2)
    along = lax.rem(home // 2, Z)
    line = [(home_at(across, lax.rem(along + d, Z)), member) for d in range(1, Z)]
    spots = [lax.rem(across + d, W) for d in range(1, W)]
    plane = [(spot, (home_at(spot, along), member)) for spot in spots]
    return line, plane, across, along


def refine(gram, right, chosen):
    steps = [1.0 / jnp.max(jnp.sum(jnp.abs(g), axis=1, keepdims=True), axis=0, keepdims=True) for g in gram]
    grams = [halves(g) for g in gram]
    fits = list(chosen)
    for _ in range(STEPS):
        updates = [r - dot3(g, halves(f), NN) for g, r, f in zip(grams, right, fits)]
        fits = [f + s * u for f, s, u in zip(fits, steps, updates)]
    return fits


def chosen_columns(row, count):
    position = lax.broadcasted_iota(jnp.int32, (2 * SLOTS, SLOTS), 0)
    slot = lax.broadcasted_iota(jnp.int32, (2 * SLOTS, SLOTS), 1)
    return jnp.where((position == row) & (slot < count), 1.0, 0.0).astype(F32)


def normal(square_matrix, columns):
    picks = columns.T
    picks16 = picks.astype(BF16)
    columns16 = columns.astype(BF16)
    high, low = halves(square_matrix)
    right = dot(picks16, high, NN) + dot(picks16, low, NN)
    high, low = halves(right)
    gram = dot(high, columns16, NN) + dot(low, columns16, NN)
    return gram, right, picks


def couple(col, row):
    total = None
    for axis in range(3):
        offset = col[axis] - row[axis]
        total = offset * offset + (1024.0 * 0.01 if total is None else total)
    return lax.rsqrt(total)


SCRATCH = [
    ("skeleton_one", (BOXES, SLOTS), jnp.int32),
    ("skeleton_two", (8, SLOTS), jnp.int32),
    ("window", (3 * BOXES, 4, PANELS), F32),
    ("column", (2, 3, PANELS, SLOTS), F32),
    ("couples", (MINE + 2, 2 * PANELS, NEAR * PANELS), BF16),
    ("siblings", (MINE // 2, 2 * PANELS, PANELS), BF16),
    ("fit_high", (MINE, SLOTS, PANELS), BF16),
    ("fit_low", (MINE, SLOTS, PANELS), BF16),
    ("left_high", (MINE, SLOTS, NEAR * PANELS), BF16),
    ("left_low", (MINE, SLOTS, NEAR * PANELS), BF16),
    ("reach", (10 * MINE, SLOTS, PANELS), F32),
    ("via", (MINE, SLOTS, PANELS), F32),
    ("round", (SLOTS, PANELS), F32),
    ("blocks", (MINE, PANELS, PANELS), F32),
    ("block", (MINE, SLOTS, SLOTS), F32),
    ("pair", (MINE // 2, SLOTS, SLOTS), F32),
    ("cross_high", (MINE, SLOTS, NEAR * SLOTS), BF16),
    ("cross_low", (MINE, SLOTS, NEAR * SLOTS), BF16),
    ("one", (MINE, SLOTS, SLOTS), F32),
    ("merged", (MINE // 2, PANELS, PANELS), F32),
    ("two", (MINE // 2, SLOTS, SLOTS), F32),
    ("mine", (16, SLOTS), F32),
    ("line_tables", (Z, 16, SLOTS), F32),
    ("ours", (8, SLOTS), jnp.int32),
    ("plane_tables", (W, 8, SLOTS), jnp.int32),
    ("answers", (W, 16, SLOTS), F32),
    ("heard", (W, 16, SLOTS), F32),
    ("lines00", (Z, MEMBERS, ROWS // 2, SLOTS), F32),
    ("lines01", (Z, MEMBERS, ROWS // 2, SLOTS), F32),
    ("lines10", (Z, MEMBERS, ROWS // 2, SLOTS), F32),
    ("lines11", (Z, MEMBERS, ROWS // 2, SLOTS), F32),
    ("packed", (2, W, 8, ROWS // 2, SLOTS), F32),
]
COPIES = [
    ("own", (9,)), ("stage", (2,)),
    ("halo_send", (2, 4)), ("halo_recv", (2, 4)),
    ("send", (7, MINE)), ("recv", (6, MINE)), ("give", (5, MINE)), ("take", (5, MINE)),
    ("table_send", (2, 7)), ("table_recv", (2, 7)), ("answer_send", (7,)), ("answer_recv", (7,)),
    ("row_send", (3,)), ("row_recv", (3,)), ("block_send", (4, 3)), ("block_recv", (4, 3)),
    ("up_send", (4, 4)), ("up_recv", (4, 4)), ("down_send", (4, 4)), ("down_recv", (4, 4)),
    ("plane_send", (2, 7)), ("plane_recv", (2, 7)),
]


class Refs:
    def __init__(self, refs):
        names = ["near", "owners"] + [name for name, *_ in SCRATCH] + [name + "_sem" for name, _ in COPIES]
        for name, ref in zip(names, refs, strict=True):
            setattr(self, name, ref)


def kernel(
    panels, self_blocks, neighbors, skeleton_one, count_one, skeleton_two, count_two, parent_at_slot, one_out, arrived, *refs
):
    v = Refs(refs)
    home, member = place()
    first = member * MINE
    boxes = range(MINE)
    side_hi, core = member // 2, lax.rem(member, 2)
    side_lo = lax.rem(home, 2)
    sign = 1 - 2 * side_hi
    outer = side_lo == side_hi
    flipped = home + 1 - 2 * side_lo
    side = (flipped, member)
    cross = (flipped, 2 * (1 - side_hi) + core)
    above = (lax.rem(home + 2 * sign + HOMES, HOMES), member)
    below = (lax.rem(home - 2 * sign + HOMES, HOMES), member)
    after = (lax.rem(home + 1, HOMES), member)
    before = (lax.rem(home + HOMES - 1, HOMES), member)
    sibling = (home, 2 * side_hi + 1 - core)
    members = [(home, lax.rem(member + d, MEMBERS)) for d in range(1, MEMBERS)]
    line, plane, across, along = lines_of(home, member)

    barrier = pltpu.get_barrier_semaphore()
    peers = [after, before, cross, above, below] + members + line + [peer for _, peer in plane]
    for peer in peers:
        pl.semaphore_signal(barrier, inc=1, device_id=peer, device_id_type=MESH)

    stage_near = pltpu.make_async_copy(neighbors, v.near, v.own_sem.at[0])
    stage_blocks = pltpu.make_async_copy(self_blocks.at[pl.ds(first, MINE)], v.blocks, v.own_sem.at[1])
    stage_panels = pltpu.make_async_copy(panels, v.window.at[pl.ds(BOXES, BOXES)], v.own_sem.at[2])
    stage_two = pltpu.make_async_copy(skeleton_two, v.skeleton_two, v.stage_sem.at[0])
    stage_one = pltpu.make_async_copy(skeleton_one, v.skeleton_one, v.stage_sem.at[1])
    for copy in (stage_near, stage_panels, stage_two, stage_one, stage_blocks):
        copy.start()

    pl.semaphore_wait(barrier, len(peers))

    def halo(way, piece):
        boxes_of = pl.ds(MINE * piece, MINE)
        room = pl.ds(2 * BOXES * way + MINE * piece, MINE)
        return send(
            panels.at[boxes_of],
            v.window.at[room],
            v.halo_send_sem.at[way, piece],
            v.halo_recv_sem.at[way, piece],
            (after, before)[way],
        )

    def halos(act):
        for piece in range(MEMBERS):
            pl.when(piece >= member)(lambda: act(halo(0, piece)))
            pl.when(piece <= member)(lambda: act(halo(1, piece)))

    halos(lambda copy: copy.start())

    lane = lax.broadcasted_iota(jnp.int32, (1, SLOTS), 1)
    nothing = jnp.full((1, SLOTS), -1.0, F32)
    owner_row, count_row, plain_row = nothing, nothing, jnp.zeros((1, SLOTS), jnp.int32)
    for s in range(8):
        owner_row = jnp.where(lane == 8 * along + s, parent_at_slot[s].astype(F32), owner_row)
        plain_row = jnp.where(lane == s, parent_at_slot[s], plain_row)
        count_row = jnp.where(lane == 8 * along + s, count_two[s].astype(F32), count_row)
    stage_two.wait()
    v.mine[0:8, :] = v.skeleton_two[...].astype(F32)
    v.mine[8:9, :] = owner_row
    v.mine[9:10, :] = count_row
    v.mine[10:16, :] = jnp.zeros((6, SLOTS), F32)
    v.ours[...] = jnp.broadcast_to(plain_row, (8, SLOTS))

    spots = [(v.mine, v.line_tables.at[along]), (v.ours, v.plane_tables.at[across])]
    stage_tables = [pltpu.make_async_copy(*spot, v.own_sem.at[3 + i]) for i, spot in enumerate(spots)]
    tables = [
        send(*spots[way], v.table_send_sem.at[way, i], v.table_recv_sem.at[way, i], peer)
        for way, peers in enumerate((line, [peer for _, peer in plane]))
        for i, peer in enumerate(peers)
    ]
    answers = [
        send(v.answers.at[at], v.heard.at[across], v.answer_send_sem.at[i], v.answer_recv_sem.at[i], peer)
        for i, (at, peer) in enumerate(plane)
    ]
    listing = pltpu.make_async_copy(v.plane_tables.at[:, 0], v.owners, v.own_sem.at[5])

    def answer():
        for copy in tables:
            copy.wait_recv()
        for copy in stage_tables:
            copy.wait()
        listing.start()
        owner_row = jnp.max(v.line_tables[:, 8, :], axis=0, keepdims=True)
        count_row = jnp.max(v.line_tables[:, 9, :], axis=0, keepdims=True)
        row = lax.broadcasted_iota(jnp.int32, (8 * W, SLOTS), 0)
        at = row >> 3
        parent = 8 * ((at >> 1) * 16 + along * 2 + (at & 1)) + (row & 7)
        found = jnp.where(owner_row == parent.astype(F32), 1.0, 0.0).astype(F32)
        skeletons = jnp.concatenate([v.line_tables[z, 0:8, :] for z in range(Z)], axis=0)
        skeletons = jnp.concatenate([skeletons, jnp.zeros_like(skeletons)], axis=0)
        chosen = dot(found.astype(BF16), skeletons.astype(BF16), NN)
        counts = jnp.broadcast_to(jnp.sum(found * count_row, axis=1, keepdims=True), chosen.shape)
        for at in range(W):
            v.answers[at, 0:8, :] = chosen[8 * at : 8 * at + 8, :]
            v.answers[at, 8:16, :] = counts[8 * at : 8 * at + 8, :]
        v.heard[across] = v.answers[across]
        begin(answers)

    def begin(copies):
        for copy in copies:
            copy.start()

    begin(tables + stage_tables)

    def slot(shift, k, to=1):
        return v.reach.at[MINE * (2 * (2 + to * sign * shift) + core) + k]

    def moved(source, target, stream, k, peer, recv):
        return send(source, target, v.send_sem.at[stream, k], v.recv_sem.at[recv, k], peer)

    def passed(shift, i, k):
        return send(slot(shift, k), slot(shift, k), v.give_sem.at[i, k], v.take_sem.at[i, k], sibling)

    def arrival(stream, k):
        return moved(slot(0, k), slot(0, k), stream, k, side, stream)

    def at_outer(body):
        pl.when(outer)(body)

    def at_inner(body):
        pl.when(jnp.logical_not(outer))(body)

    def outer_moves(k):
        return {
            "own": [
                moved(slot(0, k), slot(-2, k), 0, k, side, 0),
                moved(slot(0, k), v.via.at[k], 1, k, below, 1),
            ]
            + ([moved(slot(0, k), v.round, 5, k, cross, 5)] if k == ROUND else []),
            "side": [moved(slot(2, k), slot(-2, k), 2, k, above, 2)]
            + ([moved(slot(2, k), slot(1, k, -1), 4, k, cross, 4)] if k == OTHER else []),
            "next": [moved(v.via.at[k], slot(-1, k, -1), 3, k, cross, 3)]
            + ([moved(v.round, slot(1, k), 6, k, side, 2)] if k == ROUND else []),
        }

    def inner_moves(k):
        return {
            "own": [
                moved(slot(0, k), slot(2, k), 0, k, side, 0),
                moved(slot(0, k), slot(-1, k, -1), 1, k, cross, 1),
            ],
            "side": ([moved(slot(-2, k), slot(1, k, -1), 2, k, cross, 2)] if k != ROUND else [])
            + [moved(slot(-2, k), slot(2, k), 3, k, below, 3)],
            "next": [moved(slot(-1, k), slot(1, k), 4, k, side, 4)] if k != OTHER else [],
        }

    def send_own(k):
        at_outer(lambda: begin(outer_moves(k)["own"]))
        at_inner(lambda: begin(inner_moves(k)["own"]))
        passed(0, 4, k).start()

    def early(k):
        @at_outer
        def _():
            arrival(0, k).wait_recv()
            begin(outer_moves(k)["side"] + [passed(2, 0, k)])
            arrival(1, k).wait_recv()
            if k == ROUND:
                arrival(5, k).wait_recv()
            begin(outer_moves(k)["next"])

        @at_inner
        def _():
            arrival(0, k).wait_recv()
            begin(inner_moves(k)["side"] + [passed(-2, 0, k)])
            arrival(1, k).wait_recv()
            begin(inner_moves(k)["next"] + [passed(-1, 1, k)])

    def late(k):
        @at_outer
        def _():
            for stream, shift, i in ((2, -2, 1), (3, -1, 2), (4, 1, 3)):
                arrival(stream, k).wait_recv()
                passed(shift, i, k).start()

        @at_inner
        def _():
            for stream, shift, i in ((2, 1, 2), (3, 2, 3)):
                arrival(stream, k).wait_recv()
                passed(shift, i, k).start()

    def taken():
        for k in boxes:
            for i in range(5):
                passed(0, i, k).wait_recv()

    def sent():
        for k in boxes:

            @at_outer
            def _():
                for copies in outer_moves(k).values():
                    for copy in copies:
                        copy.wait_send()

            @at_inner
            def _():
                for copies in inner_moves(k).values():
                    for copy in copies:
                        copy.wait_send()

            for i in range(5):
                passed(0, i, k).wait_send()

    tile = 64

    def columns_of(box, turn):
        for axis in range(3):
            row = 32.0 * v.window[BOXES + box, axis : axis + 1, :]
            v.column[turn, axis] = jnp.broadcast_to(row, (SLOTS, PANELS)).T

    def couple_with(turn, box, target, first_lane):
        for part in range(PANELS // SLOTS):
            lanes = slice(part * SLOTS, (part + 1) * SLOTS)
            row = [32.0 * v.window[box, axis : axis + 1, lanes] for axis in range(3)]
            lanes = slice(first_lane + part * SLOTS, first_lane + (part + 1) * SLOTS)
            for start in range(0, PANELS, tile):
                col = [v.column[turn, axis, start : start + tile, :] for axis in range(3)]
                hi, lo = halves(couple(col, row))
                target[start : start + tile, lanes] = hi
                target[PANELS + start : PANELS + start + tile, lanes] = lo

    order = [(first + k, slot(0, k), k) for k in boxes]

    def proxies(i, indices):
        box, _, room = order[i]
        for index in indices:
            near = within(v.near[index, box] - (home - 1) * BOXES, 3 * BOXES)
            couple_with(i % 2, near, v.couples.at[room], index * PANELS)

    def products(room, half):
        lanes = slice(half * (NEAR * PANELS // 2), (half + 1) * (NEAR * PANELS // 2))
        return dot(v.couples[room, :, lanes], v.couples[room, :PANELS, lanes], NT)

    def fit_box(i):
        box, spot, room = order[i]
        more = 0 < i < len(order) - 1
        if more:
            columns_of(order[i + 1][0], (i + 1) % 2)
        total = products(room, 0)
        if more:
            proxies(i + 1, (0, 1, 2))
        total = total + products(room, 1)
        if more:
            proxies(i + 1, (3, 4, 5))
        low = total[PANELS:]
        columns = chosen_columns(v.skeleton_one[pl.ds(box, 1), :], count_one[box])
        gram, right, pick = normal(total[:PANELS] + (low + low.T), columns)
        (fit,) = refine([gram], [right], [pick])
        if more:
            proxies(i + 1, (6, 7))
        weight = jnp.sum(fit * fit * v.window[BOXES + box, 3:4, :], axis=1, keepdims=True)
        spot[...] = fit * lax.rsqrt(jnp.maximum(weight, 1.0))
        if i < MINE:
            v.fit_high[i], v.fit_low[i] = halves(fit)

    def split_fit(own):
        return v.fit_high[own], v.fit_low[own]

    def left_box(own):
        for index in range(NEAR):
            lanes = slice(index * PANELS, (index + 1) * PANELS)
            product = dot3(split_fit(own), (v.couples[own, :PANELS, lanes], v.couples[own, PANELS:, lanes]), NN)
            v.left_high[own, :, lanes], v.left_low[own, :, lanes] = halves(product)
        part = dot3(split_fit(own), halves(v.blocks[own]), NN)
        v.block[own] = dot3(halves(part), split_fit(own), NT)

    def pair_of(j):
        a, e = 2 * j, 2 * j + 1
        columns_of(first + a, j)
        couple_with(j, BOXES + first + e, v.siblings.at[j], 0)
        part = dot3(split_fit(a), (v.siblings[j, :PANELS, :], v.siblings[j, PANELS:, :]), NN)
        v.pair[j] = dot3(halves(part), split_fit(e), NT)

    stage_near.wait()
    stage_one.wait()
    stage_panels.wait()
    halos(lambda copy: copy.wait_recv())
    columns_of(first, 0)
    proxies(0, range(NEAR))
    fit_box(0)
    send_own(0)
    columns_of(first + 1, 1)
    proxies(1, range(NEAR))
    fit_box(1)
    send_own(1)
    early(0)
    answer()
    fit_box(2)
    send_own(2)
    early(1)
    fit_box(3)
    send_own(3)
    early(2)
    late(0)
    stage_blocks.wait()
    left_box(0)
    late(1)
    early(3)
    left_box(1)
    pair_of(0)
    late(2)
    left_box(2)
    left_box(3)
    pair_of(1)
    late(3)
    taken()

    base = 16 * home + 8 * side_hi - 16

    def level_one(own):
        for index in range(NEAR):
            box = within(v.near[index, first + own] - base, 10 * MINE)
            lanes = slice(index * PANELS, (index + 1) * PANELS)
            left = (v.left_high[own, :, lanes], v.left_low[own, :, lanes])
            lanes = slice(index * SLOTS, (index + 1) * SLOTS)
            v.cross_high[own, :, lanes], v.cross_low[own, :, lanes] = halves(dot3(left, halves(v.reach[box]), NT))
        v.one[own] = v.block[own] - square((v.cross_high[own], v.cross_low[own]), NT)

    def level_two(j):
        between = v.pair[j]
        v.merged[j, :SLOTS, :SLOTS] = v.one[2 * j]
        v.merged[j, :SLOTS, SLOTS:] = between
        v.merged[j, SLOTS:, :SLOTS] = between.T
        v.merged[j, SLOTS:, SLOTS:] = v.one[2 * j + 1]
        body = halves(v.merged[j])
        which = 2 * member + j
        row, count = v.heard[0, pl.ds(which, 1), :], v.heard[0, pl.ds(8 + which, 1), :]
        for at in range(1, W):
            row = row + v.heard[at, pl.ds(which, 1), :]
            count = count + v.heard[at, pl.ds(8 + which, 1), :]
        columns = chosen_columns(row.astype(jnp.int32), count.astype(jnp.int32))
        gram, right, pick = normal(square(body, TN), columns)
        (fit,) = refine([gram], [right], [pick])
        fit = halves(fit)
        v.two[j] = dot3(halves(dot3(fit, body, NN)), fit, NT)

    mine_one = one_out.at[pl.ds(MINE * member, MINE)]

    def one_rows(target):
        return v.one.at[:, pl.ds(pl.multiple_of(target * ROWS, ROWS), ROWS), :]

    own_one = pltpu.make_async_copy(one_rows(member), mine_one, v.own_sem.at[6])
    ones = [
        send(one_rows(peer[1]), mine_one, v.row_send_sem.at[i], v.row_recv_sem.at[i], peer)
        for i, peer in enumerate(members)
    ]

    up, down = line[0], line[-1]
    half = ROWS // 2
    lines = ((v.lines00, v.lines01), (v.lines10, v.lines11))

    def two_rows(j, part, target):
        return v.two.at[j, pl.ds(pl.multiple_of(target * ROWS + part * half, half), half), :]

    def member_copies(j, part):
        spot = lines[j][part].at[along, member]
        return [
            send(
                two_rows(j, part, peer[1]),
                spot,
                v.block_send_sem.at[2 * j + part, i],
                v.block_recv_sem.at[2 * j + part, i],
                peer,
            )
            for i, peer in enumerate(members)
        ]

    def upward(j, part, step):
        spot = lines[j][part].at[lax.rem(along - step + Z, Z)]
        return send(spot, spot, v.up_send_sem.at[2 * j + part, step], v.up_recv_sem.at[2 * j + part, step], up)

    def downward(j, part, step):
        spot = lines[j][part].at[lax.rem(along + step, Z)]
        return send(spot, spot, v.down_send_sem.at[2 * j + part, step], v.down_recv_sem.at[2 * j + part, step], down)

    def ways(part):
        return ((upward, 4), (downward, 3)) if part == 0 else ((upward, 3), (downward, 4))

    def share(j):
        for part in range(2):
            lines[j][part][along, member] = v.two[
                j, pl.ds(pl.multiple_of(member * ROWS + part * half, half), half), :
            ]
            begin(member_copies(j, part))

    def gather(j, part, step):
        if step == 0:
            for copy in member_copies(j, part):
                copy.wait_recv()
        for copy, count in ways(part):
            if 0 < step <= count:
                copy(j, part, step - 1).wait_recv()
            if step < count:
                copy(j, part, step).start()

    def pack(part, at):
        for s in range(8):
            parent = v.owners[at, s]
            z, m = lax.rem(parent // 16, Z), lax.rem(parent // 2, MEMBERS)
            odd = lax.rem(parent, 2)
            v.packed[part, at, s] = jnp.where(odd == 1, lines[1][part][z, m], lines[0][part][z, m])

    def across_copy(part, i):
        at, peer = plane[i]
        return send(
            v.packed.at[part, at],
            arrived.at[part, across],
            v.plane_send_sem.at[part, i],
            v.plane_recv_sem.at[part, i],
            peer,
        )

    own_across = [
        pltpu.make_async_copy(v.packed.at[part, across], arrived.at[part, across], v.own_sem.at[7 + part])
        for part in range(2)
    ]

    def send_across(part):
        for i, (at, _) in enumerate(plane):
            pack(part, at)
            across_copy(part, i).start()
        pack(part, across)
        own_across[part].start()

    for copy in answers:
        copy.wait_recv()
    level_one(0)
    level_one(1)
    level_two(0)
    share(0)
    level_one(2)
    level_one(3)
    level_two(1)
    share(1)
    begin(ones + [own_one])
    listing.wait()
    gather(0, 0, 0)
    gather(1, 0, 0)
    gather(0, 0, 1)
    gather(1, 0, 1)
    gather(0, 1, 0)
    gather(1, 1, 0)
    gather(0, 0, 2)
    gather(1, 0, 2)
    gather(0, 1, 1)
    gather(1, 1, 1)
    gather(0, 0, 3)
    gather(1, 0, 3)
    gather(0, 1, 2)
    gather(1, 1, 2)
    gather(0, 0, 4)
    gather(1, 0, 4)
    send_across(0)
    gather(0, 1, 3)
    gather(1, 1, 3)
    gather(0, 1, 4)
    gather(1, 1, 4)
    send_across(1)

    for part in range(2):
        for i in range(W - 1):
            across_copy(part, i).wait()
    for copy in own_across + [own_one] + ones:
        copy.wait()
    sent()
    halos(lambda copy: copy.wait_send())
    for copy in tables + answers:
        copy.wait_send()
    for j in range(2):
        for part in range(2):
            for copy in member_copies(j, part):
                copy.wait_send()
            for copy, count in ways(part):
                for step in range(count):
                    copy(j, part, step).wait_send()


def place_kernel(owners, one, arrived, one_out, two_out, sems):
    copies = [pltpu.make_async_copy(one, one_out, sems.at[16])]
    for s in range(8):
        source = owners[s] // 8
        at = 2 * (source // 16) + lax.rem(source, 2)
        for part in range(2):
            half = ROWS // 2
            copies.append(
                pltpu.make_async_copy(
                    arrived.at[part, at, s], two_out.at[s, pl.ds(part * half, half), :], sems.at[2 * s + part]
                )
            )
    for copy in copies:
        copy.start()
    for copy in copies:
        copy.wait()


def local(panels, self_blocks, neighbors, skeleton_one, count_one, skeleton_two, count_two, parent_at_slot):
    hbm = pl.BlockSpec(memory_space=pl.ANY)
    vmem = pl.BlockSpec(memory_space=pltpu.VMEM)
    smem = pl.BlockSpec(memory_space=pltpu.SMEM)
    one, arrived = pl.pallas_call(
        kernel,
        out_shape=[
            jax.ShapeDtypeStruct((BOXES, ROWS, SLOTS), F32),
            jax.ShapeDtypeStruct((2, W, 8, ROWS // 2, SLOTS), F32),
        ],
        in_specs=[hbm, hbm, hbm, hbm, smem, hbm, smem, smem],
        out_specs=[hbm, hbm],
        scratch_shapes=[
            pltpu.SMEM((NEAR, BOXES), jnp.int32),
            pltpu.SMEM((W, SLOTS), jnp.int32),
            *(pltpu.VMEM(shape, dtype) for _, shape, dtype in SCRATCH),
            *(pltpu.SemaphoreType.DMA(shape) for _, shape in COPIES),
        ],
        compiler_params=pltpu.CompilerParams(collective_id=0, has_side_effects=True, vmem_limit_bytes=56 * MIB),
        name="skeletonize",
    )(panels, self_blocks, neighbors.T, skeleton_one, count_one, skeleton_two, count_two, parent_at_slot)
    return pl.pallas_call(
        place_kernel,
        out_shape=[
            jax.ShapeDtypeStruct((BOXES, ROWS, SLOTS), F32),
            jax.ShapeDtypeStruct((8, ROWS, SLOTS), F32),
        ],
        in_specs=[smem, hbm, hbm],
        out_specs=[vmem, vmem],
        scratch_shapes=[pltpu.SemaphoreType.DMA((17,))],
        compiler_params=pltpu.CompilerParams(vmem_limit_bytes=56 * MIB),
        name="place",
    )(parent_at_slot, one, arrived)


def solution(mesh):
    placed = (
        P("box", None, None),
        P("box", None, None),
        P("box", None),
        P("box", None),
        P("box"),
        P("box", None),
        P("box"),
        P("box"),
    )
    return jax.shard_map(
        local,
        mesh=mesh,
        in_specs=placed,
        out_specs=(P("box", "blk", None), P("box", "blk", None)),
        check_vma=False,
    )
```
